32 devices in a mesh: parts: 2 (over y), aux: 4 (over z), bas: 2 (over x), occ: 2 (over core).
Axes of the slice: x: 2, y: 2, z: 4, core: 2. Of those that a mesh axis runs over, the one named last changes fastest.
Arguments:
- integrals: bfloat16 [8, 2, 2, 128, 128, 128], P(('parts', 'aux'), 'bas'), parts along dimension 0
- screening: int32 [8, 2, 2], P(('parts', 'aux'), 'bas'), parts along dimension 0, may hold values from 0 to 15, as said below
- coefficients: bfloat16 [4096, 256], P(('parts', 'bas'), 'occ'), parts along dimension 0, may hold values from -0.375 to 0.375
- metric: bfloat16 [1024, 512], P(('parts', 'aux')), parts along dimension 0
- aux_owner: int32 [8], P('parts'), parts along dimension 0, may hold values from 0 to 3, each once
Outputs:
- exchange: float32 [512, 256], P(('parts', 'bas'), ('aux', 'occ')), parts along dimension 0
The draws below stay inside these ranges and needn't reach their ends.
There are 2 independent parts, one for each index of `parts`. The reference program is written for one: setup_inputs(seed, part) draws one part's arguments, and reference() takes and returns one part's arrays. A program takes and returns all parts, laid end to end along the dimension named above; each array names one. Nothing has to cross between parts.
Inputs may be any that keep to these rules, and one draw needn't show every extreme that they name: `screening`: each aux and bas index holds 2 distinct contracted blocks, consecutive modulo 16. `aux_owner`: a permutation.
All inputs are finite; a program needn't handle non-finite values.
Results may differ from the reference program's by a relative error of at most 0.0003.
Values may be sent and summed in bfloat16 or wider, within the bound.
No kernel may reach another device: no remote copies, remote signals or barrier semaphores. Data moves between devices by JAX's collectives and lax.ppermute only.
A program may use at most 128 MiB of HBM per device.

```python
import jax
import jax.numpy as jnp

BLK = 128
NOCC = 256
SLOTS = 2
NCB = 16
NAUX = 512
NBW = 256
N_AUX = 4
N_BAS = 2


def draw_integrals(key, part):
    key = jax.random.fold_in(key, 11)
    first = jax.random.fold_in(key, 0)
    shape = (N_AUX, N_BAS, SLOTS, BLK, BLK, BLK)
    noise = jax.random.normal(first, shape, jnp.float32)
    mixed = (noise + 0.7 * jnp.roll(noise, -1, axis=-1)) * (1.0 / 1.49 ** 0.5)
    return mixed.astype(jnp.bfloat16)


def draw_screening(key, part):
    key = jax.random.fold_in(key, 12)
    starts = jax.random.randint(key, (N_AUX * N_BAS,), 0, NCB)
    starts = starts.at[0].set(NCB - SLOTS).at[1].set(0)
    offsets = jnp.arange(SLOTS, dtype=jnp.int32)
    blocks = (starts[:, None] + offsets[None, :]) % NCB
    return blocks.reshape(N_AUX, N_BAS, SLOTS).astype(jnp.int32)


def draw_metric(key, part):
    key = jax.random.fold_in(key, 13)
    first, second = jax.random.split(key)
    diagonal = jax.random.uniform(first, (NAUX,), jnp.float32, 0.5, 1.5)
    spread = jax.random.normal(second, (NAUX, NAUX), jnp.float32) * (0.5 / NAUX ** 0.5)
    rows = jnp.arange(NAUX)[:, None]
    cols = jnp.arange(NAUX)[None, :]
    matrix = jnp.where(rows == cols, diagonal[:, None] + spread, spread)
    return (matrix / (NAUX * NOCC) ** 0.5).astype(jnp.bfloat16)


def level_of(rng, dims, shards, low, top_value):
    factor_of, own = 1.0, jax.random.fold_in(rng, 6)
    for position, parts in shards:
        steps = jnp.exp(jax.random.uniform(jax.random.fold_in(own, position), (parts,), jnp.float32, low / len(shards), top_value / len(shards)))
        factor_of = factor_of * jnp.repeat(steps, dims[position] // parts).reshape([-1 if axis == position else 1 for axis in range(len(dims))])
    return factor_of


def scatter_about(stream_key, dims, scale, limit, pieces=(), kind=jnp.bfloat16):
    loudness = level_of(stream_key, dims, pieces, -0.22, 0.18) if pieces else 1.0
    values = jax.random.normal(stream_key, dims, jnp.float32) * scale * loudness
    return jnp.minimum(jnp.maximum(values, -limit), limit).astype(kind)


def setup_inputs(seed: int = 0, part: int = 0) -> dict:
    key_list = jax.random.split(jax.random.key(seed), 6)
    own_keys = jax.random.split(jax.random.fold_in(key_list[5], part), 6)
    return {
        "integrals": draw_integrals(jax.random.fold_in(jax.random.fold_in(key_list[5], part), 71), part),
        "screening": draw_screening(jax.random.fold_in(jax.random.fold_in(key_list[5], part), 71), part),
        "coefficients": scatter_about(own_keys[2], (NCB * BLK, NOCC), (SLOTS * BLK) ** -0.5, 0.375, ((0, 2), (1, 2))),
        "metric": draw_metric(jax.random.fold_in(jax.random.fold_in(key_list[5], part), 71), part),
        "aux_owner": jax.random.permutation(own_keys[4], N_AUX).astype(jnp.int32),
    }


def reference(integrals, screening, coefficients, metric, aux_owner):
    by_block = coefficients.reshape(NCB, BLK, NOCC).astype(jnp.float32)
    picked = by_block[screening]
    half = jnp.einsum("absnpm,absni->iapbm", integrals.astype(jnp.float32), picked).astype(jnp.bfloat16)
    columns = metric.reshape(NAUX, N_AUX, BLK)[:, aux_owner, :].astype(jnp.float32)
    fitted = jnp.einsum("qap,iapbm->iqbm", columns, half.astype(jnp.float32)).astype(jnp.bfloat16)
    wide = fitted.astype(jnp.float32)
    inner = jnp.einsum("iqbm,iqcn->bmcn", wide, wide)
    return inner.reshape(NBW, NBW)
```

```python
import functools

import jax
import jax.numpy as jnp
from jax import lax
from jax.experimental import pallas as pl
from jax.experimental.pallas import tpu as pltpu
from jax.sharding import PartitionSpec as P

F32 = jnp.float32
BF16 = jnp.bfloat16
ROWS = 16
WHOLE = pl.BlockSpec(memory_space=pltpu.VMEM)


def params(mib=40):
    return pltpu.CompilerParams(vmem_limit_bytes=mib * 2**20)


def cost(macs, size):
    return pl.CostEstimate(flops=2 * macs, bytes_accessed=size, transcendentals=0)


def relayout_kernel(x_ref, o_ref):
    slots, depth, rows, width = x_ref.shape
    o_ref[...] = jnp.swapaxes(x_ref[...].reshape(slots * depth, rows, width), 0, 1)


def relayout(integrals, first):
    slots, depth, _, width = integrals.shape
    return pl.pallas_call(
        relayout_kernel,
        grid=(first // ROWS,),
        in_specs=[pl.BlockSpec((slots, depth, ROWS, width), lambda j: (0, 0, j, 0))],
        out_specs=pl.BlockSpec((ROWS, slots * depth, width), lambda j: (j, 0, 0)),
        out_shape=jax.ShapeDtypeStruct((first, slots * depth, width), BF16),
        compiler_params=params(),
        cost_estimate=cost(0, 2 * first * slots * depth * width * 2),
        name="relayout",
    )(integrals)


def products(table, block):
    parts = []
    for p in range(0, block.shape[0], 2):
        pair = jnp.concatenate([block[p], block[p + 1]], axis=1)
        value = jnp.dot(table, pair, preferred_element_type=F32).astype(BF16)
        width = block.shape[2]
        parts += [value[:, :width], value[:, width:]]
    return jnp.swapaxes(jnp.stack(parts), 0, 1)


def first_kernel(chips, where, own_ref, other_ref, x_ref, *rest):
    outs, table_ref, plain = rest[:chips], rest[chips], rest[chips + 1]
    share = table_ref.shape[0] // chips

    @pl.when(pl.program_id(0) == 0)
    def _():
        block = plain.shape[0]
        held = own_ref.shape[0] // block
        for s in range(plain.shape[1] // block):
            name = where[2 + s]
            away = lax.div(name, held) != where[1]
            start = pl.multiple_of(lax.rem(name, held) * block, block)
            mine = own_ref[pl.ds(start, block), :].astype(F32)
            theirs = other_ref[pl.ds(start, block), :].astype(F32)
            picked = jnp.where(away, theirs, mine)
            plain[:, s * block : (s + 1) * block] = picked.T.astype(BF16)
        for k in range(chips):
            start = pl.multiple_of((where[0] ^ k) * share, share)
            table_ref[k * share : (k + 1) * share, :] = plain[pl.ds(start, share), :]

    value = products(table_ref[...], x_ref[...])
    for k in range(chips):
        outs[k][...] = value[k * share : (k + 1) * share]


def first_products(chips, where, own, other, moved):
    first, depth, width = moved.shape
    orbitals = own.shape[1]
    share = orbitals // chips
    whole = lambda shape: pl.BlockSpec(shape, lambda j, w: (0,) * len(shape))
    return pl.pallas_call(
        functools.partial(first_kernel, chips),
        grid_spec=pltpu.PrefetchScalarGridSpec(
            num_scalar_prefetch=1,
            grid=(first // ROWS,),
            in_specs=[
                whole(own.shape),
                whole(other.shape),
                pl.BlockSpec((ROWS, depth, width), lambda j, w: (j, 0, 0)),
            ],
            out_specs=[pl.BlockSpec((share, ROWS, width), lambda j, w: (0, j, 0))] * chips
            + [whole((orbitals, depth))],
            scratch_shapes=[pltpu.VMEM((orbitals, depth), BF16)],
        ),
        out_shape=[jax.ShapeDtypeStruct((share, first, width), BF16)] * chips
        + [jax.ShapeDtypeStruct((orbitals, depth), BF16)],
        compiler_params=params(),
        cost_estimate=cost(orbitals * depth * first * width, moved.size * 2),
        name="first_products",
    )(where, own, other, moved)


def rest_kernel(chips, groups, x_ref, table_ref, *outs):
    slots, depth, rows, width = x_ref.shape
    block = jnp.swapaxes(x_ref[...].reshape(slots * depth, rows, width), 0, 1)
    value = products(table_ref[...], block)
    share = table_ref.shape[0] // chips
    for g, (lo, hi) in enumerate(groups):
        for k in range(chips):
            outs[g * chips + k][...] = value[k * share + lo : k * share + hi]


def rest_products(chips, groups, integrals, table, first):
    slots, depth, total, width = integrals.shape
    orbitals = table.shape[0]
    rest = total - first
    skip = first // ROWS
    shapes = [(hi - lo) for lo, hi in groups for _ in range(chips)]
    return pl.pallas_call(
        functools.partial(rest_kernel, chips, groups),
        grid=(rest // ROWS,),
        in_specs=[
            pl.BlockSpec((slots, depth, ROWS, width), lambda j: (0, 0, j + skip, 0)),
            pl.BlockSpec(table.shape, lambda j: (0, 0)),
        ],
        out_specs=[pl.BlockSpec((n, ROWS, width), lambda j: (0, j, 0)) for n in shapes],
        out_shape=[jax.ShapeDtypeStruct((n, rest, width), BF16) for n in shapes],
        compiler_params=params(),
        cost_estimate=cost(orbitals * table.shape[1] * rest * width, integrals.size * 2),
        name="rest_products",
    )(integrals, table)


def metric_kernel(where, own_ref, near_ref, far_ref, o_ref):
    aux = where.shape[0] - 1
    width = o_ref.shape[1] // aux
    for kz in range(aux):
        start = pl.multiple_of(where[where[aux] ^ kz] * width, width)
        at = 0
        for ref in (own_ref, near_ref, far_ref):
            size = ref.shape[0]
            o_ref[at : at + size, kz * width : (kz + 1) * width] = ref[:, pl.ds(start, width)]
            at += size


def ordered_metric(where, own, near, far):
    total = own.shape[0] + near.shape[0] + far.shape[0]
    return pl.pallas_call(
        metric_kernel,
        in_specs=[pl.BlockSpec(memory_space=pltpu.SMEM)] + [WHOLE] * 3,
        out_specs=WHOLE,
        out_shape=jax.ShapeDtypeStruct((total, own.shape[1]), BF16),
        compiler_params=params(),
        cost_estimate=cost(0, total * own.shape[1] * 4),
        name="ordered_metric",
    )(where, own, near, far)


def add_group(aux, bas, lo, hi, metric, early, late, total):
    chips = aux * bas
    for i in range(lo, hi):
        columns = []
        for k in range(chips):
            columns.append(jnp.concatenate([early[k][i], late[k][i - lo]], axis=0))
        stacked = jnp.concatenate(
            [jnp.concatenate(columns[kz * bas : (kz + 1) * bas], axis=1) for kz in range(aux)],
            axis=0,
        )
        fitted = jnp.dot(metric, stacked, preferred_element_type=F32).astype(BF16)
        total = total + lax.dot_general(
            fitted, fitted, (((0,), (0,)), ((), ())), preferred_element_type=F32
        )
    return total


def group_kernel(aux, bas, lo, hi, started, last, *refs):
    chips = aux * bas
    refs = list(refs)
    where = refs.pop(0) if last else None
    metric = refs.pop(0)[...]
    early = [refs.pop(0) for _ in range(chips)]
    late = [refs.pop(0) for _ in range(chips)]
    side = bas * late[0].shape[2]
    total = refs.pop(0)[...] if started else jnp.zeros((side, side), F32)
    total = add_group(aux, bas, lo, hi, metric, early, late, total)
    if not last:
        refs[0][...] = total
        return
    kept, near, away, scratch = refs
    scratch[...] = total
    width = side // bas
    piece = kept.shape[1]
    for ka in range(aux):
        a = where[0] ^ ka
        for who in range(2):
            row = (a * 2 + (where[2] ^ who)) * piece
            block = lax.div(row, width) ^ where[1]
            start = pl.multiple_of(block * width + lax.rem(row, width), piece)
            value = scratch[pl.ds(start, piece), :]
            if who:
                away[ka] = value
            else:
                kept[ka] = value[:, :width]
                near[ka] = value[:, width:]


def group(aux, bas, lo, hi, metric, early, late, total, where=None):
    last, started = where is not None, total is not None
    width = late[0].shape[2]
    side = bas * width
    args = ([where] if last else []) + [metric, *early, *late] + ([total] if started else [])
    specs = [WHOLE] * len(args)
    if last:
        specs[0] = pl.BlockSpec(memory_space=pltpu.SMEM)
        piece = side // (aux * 2)
        out = [
            jax.ShapeDtypeStruct((aux, piece, width), F32),
            jax.ShapeDtypeStruct((aux, piece, width), F32),
            jax.ShapeDtypeStruct((aux, piece, side), F32),
        ]
    else:
        out = jax.ShapeDtypeStruct((side, side), F32)
    rows = metric.shape[0]
    macs = (hi - lo) * (rows * rows * side + rows * side * side)
    return pl.pallas_call(
        functools.partial(group_kernel, aux, bas, lo, hi, started, last),
        in_specs=specs,
        out_specs=[WHOLE] * 3 if last else WHOLE,
        out_shape=out,
        scratch_shapes=[pltpu.VMEM((side, side), F32)] if last else [],
        compiler_params=params(),
        cost_estimate=cost(macs, (hi - lo) * rows * side * 2),
        name="group",
    )(*args)


def turn_kernel(*refs):
    total = refs[0][...]
    for ref in refs[1:-1]:
        total = total + ref[...]
    refs[-1][...] = total.T


def per_device(integrals, screening, coefficients, metric, aux_owner):
    aux = lax.axis_size("aux")
    bas = lax.axis_size("bas")
    chips = aux * bas
    integrals = integrals[0, 0]
    orbitals = coefficients.shape[1]
    share = orbitals // chips
    a, b, o = (lax.axis_index(name) for name in ("aux", "bas", "occ"))
    first = integrals.shape[2] // 4
    groups = ((0, 6), (6, 12), (12, share))

    def swap(value, kz=0, kx=0):
        pairs = [
            (i * bas + j, (i ^ kz) * bas + (j ^ kx)) for i in range(aux) for j in range(bas)
        ]
        return lax.ppermute(value, ("aux", "bas"), pairs)

    def across(value):
        return lax.ppermute(value, "occ", [(0, 1), (1, 0)])

    other = swap(coefficients, kx=1)
    rows = metric.shape[0] // 2
    half = lax.dynamic_slice_in_dim(metric, o * rows, rows, axis=0)
    near = jnp.concatenate([swap(half, kz=kz) for kz in range(1, aux)], axis=0)
    far = across(near)
    ordered = ordered_metric(
        jnp.concatenate([aux_owner, a[None]]).astype(jnp.int32), metric, near, far
    )

    moved = relayout(integrals, first)
    where = jnp.concatenate([jnp.stack([a * bas + b, b]), screening[0, 0]]).astype(jnp.int32)
    *early, table = first_products(chips, where, coefficients, other, moved)
    late = rest_products(chips, groups, integrals, table, first)

    order = sorted(range(1, chips), key=lambda k: -(k // bas in (2, 3)))

    def spread(values):
        got = {0: values[0]}
        for k in order:
            got[k] = swap(values[k], k // bas, k % bas)
        return [got[k] for k in range(chips)]

    early = spread(early)
    total = None
    for g, (lo, hi) in enumerate(groups):
        part = spread(late[g * chips : (g + 1) * chips])
        here = jnp.stack([a, b, o]).astype(jnp.int32) if g == len(groups) - 1 else None
        total = group(aux, bas, lo, hi, ordered, early, part, total, here)
    kept, near, away = total
    away = across(away)
    width = kept.shape[2]
    kept = kept + away[:, :, :width]
    near = near + away[:, :, width:]
    kept = kept + swap(near, kx=1)
    pieces = [kept[0]] + [swap(kept[kz], kz=kz) for kz in range(1, aux)]
    return pl.pallas_call(
        turn_kernel,
        in_specs=[WHOLE] * aux,
        out_specs=WHOLE,
        out_shape=jax.ShapeDtypeStruct((width, kept.shape[1]), F32),
        name="turn",
    )(*pieces)


def plain_device(integrals, screening, coefficients, metric, aux_owner):
    block_size = integrals.shape[-1]
    aux_count = lax.axis_size("aux")
    bas_count = lax.axis_size("bas")
    occ_count = lax.axis_size("occ")
    gathered = lax.all_gather(coefficients, "bas", axis=0, tiled=True)
    orbitals = gathered.shape[1]
    by_block = gathered.reshape(gathered.shape[0] // block_size, block_size, orbitals)
    picked = jnp.take(by_block, screening[0, 0], axis=0)
    stacked = integrals[0, 0].reshape(integrals.shape[2], block_size, block_size * block_size)
    contracted = lax.dot_general(
        picked, stacked, (((0, 1), (0, 1)), ((), ())), preferred_element_type=jnp.float32
    )
    transformed = contracted.astype(jnp.bfloat16)
    share = orbitals // (aux_count * bas_count)
    moved = lax.all_to_all(
        transformed.reshape(orbitals, 1, block_size, block_size),
        ("aux", "bas"),
        split_axis=0,
        concat_axis=1,
        tiled=True,
    )
    moved = moved.reshape(share, aux_count, bas_count, block_size, block_size)
    aux_table = (aux_owner[:, None] == jnp.arange(aux_count, dtype=jnp.int32)[None, :]).astype(
        jnp.bfloat16
    )
    piece = lax.all_gather(metric, "aux", axis=0, tiled=True)
    columns = piece.reshape(piece.shape[0], aux_count, block_size)
    ordered = jnp.einsum(
        "rgp,ag->rap", columns, aux_table, preferred_element_type=jnp.float32
    ).astype(jnp.bfloat16)
    fitted = jnp.einsum(
        "rap,iabpm->irbm", ordered, moved, preferred_element_type=jnp.float32
    ).astype(jnp.bfloat16)
    partial_value = jnp.einsum(
        "iqbm,iqcn->bmcn", fitted, fitted, preferred_element_type=jnp.float32
    )
    column_share = bas_count * block_size // (aux_count * occ_count)
    arranged = partial_value.reshape(bas_count, block_size, aux_count, occ_count, column_share)
    arranged = arranged.transpose(2, 0, 3, 1, 4).reshape(-1, column_share)
    return lax.psum_scatter(arranged, ("aux", "bas", "occ"), scatter_dimension=0, tiled=True)


def solution(mesh):
    in_specs = (
        P(("parts", "aux"), "bas", None, None, None, None),
        P(("parts", "aux"), "bas", None),
        P(("parts", "bas"), "occ"),
        P(("parts", "aux"), None),
        P("parts"),
    )
    out_specs = P(("parts", "bas"), ("aux", "occ"))
    small = mesh.shape["aux"] == 4 and mesh.shape["bas"] == 2 and mesh.shape["occ"] == 2
    return jax.shard_map(
        per_device if small else plain_device,
        mesh=mesh,
        in_specs=in_specs,
        out_specs=out_specs,
        check_vma=False,
    )
```

```python
import functools

import jax
import jax.numpy as jnp
from jax import lax
from jax.experimental import pallas as pl
from jax.experimental.pallas import tpu as pltpu
from jax.sharding import PartitionSpec as P

F32 = jnp.float32
BF16 = jnp.bfloat16
ROWS = 16
WINDOW = 5
WHOLE = pl.BlockSpec(memory_space=pltpu.VMEM)


def params(mib=40):
    return pltpu.CompilerParams(vmem_limit_bytes=mib * 2**20)


def cost(macs, size):
    return pl.CostEstimate(flops=2 * macs, bytes_accessed=size, transcendentals=0)


def relayout_kernel(x_ref, o_ref):
    slots, depth, rows, width = x_ref.shape
    o_ref[...] = jnp.swapaxes(x_ref[...].reshape(slots * depth, rows, width), 0, 1)


def relayout(integrals, first):
    slots, depth, _, width = integrals.shape
    return pl.pallas_call(
        relayout_kernel,
        grid=(first // ROWS,),
        in_specs=[pl.BlockSpec((slots, depth, ROWS, width), lambda j: (0, 0, j, 0))],
        out_specs=pl.BlockSpec((ROWS, slots * depth, width), lambda j: (j, 0, 0)),
        out_shape=jax.ShapeDtypeStruct((first, slots * depth, width), BF16),
        compiler_params=params(),
        cost_estimate=cost(0, 2 * first * slots * depth * width * 2),
        name="relayout",
    )(integrals)


def products(table, block):
    parts = []
    for p in range(0, block.shape[0], 2):
        pair = jnp.concatenate([block[p], block[p + 1]], axis=1)
        value = jnp.dot(table, pair, preferred_element_type=F32).astype(BF16)
        width = block.shape[2]
        parts += [value[:, :width], value[:, width:]]
    return jnp.swapaxes(jnp.stack(parts), 0, 1)


def first_kernel(chips, where, own_ref, other_ref, x_ref, *rest):
    outs, table_ref, plain = rest[:chips], rest[chips], rest[chips + 1]
    share = table_ref.shape[0] // chips

    @pl.when(pl.program_id(0) == 0)
    def _():
        block = plain.shape[0]
        held = own_ref.shape[0] // block
        for s in range(plain.shape[1] // block):
            name = where[2 + s]
            away = lax.div(name, held) != where[1]
            start = pl.multiple_of(lax.rem(name, held) * block, block)
            mine = own_ref[pl.ds(start, block), :].astype(F32)
            theirs = other_ref[pl.ds(start, block), :].astype(F32)
            picked = jnp.where(away, theirs, mine)
            plain[:, s * block : (s + 1) * block] = picked.T.astype(BF16)
        for k in range(chips):
            start = pl.multiple_of((where[0] ^ k) * share, share)
            table_ref[k * share : (k + 1) * share, :] = plain[pl.ds(start, share), :]

    value = products(table_ref[...], x_ref[...])
    for k in range(chips):
        outs[k][...] = value[k * share : (k + 1) * share]


def first_products(chips, where, own, other, moved, first):
    _, depth, width = moved.shape
    orbitals = own.shape[1]
    share = orbitals // chips
    whole = lambda shape: pl.BlockSpec(shape, lambda j, w: (0,) * len(shape))
    return pl.pallas_call(
        functools.partial(first_kernel, chips),
        grid_spec=pltpu.PrefetchScalarGridSpec(
            num_scalar_prefetch=1,
            grid=(first // ROWS,),
            in_specs=[
                whole(own.shape),
                whole(other.shape),
                pl.BlockSpec((ROWS, depth, width), lambda j, w: (j, 0, 0)),
            ],
            out_specs=[pl.BlockSpec((share, ROWS, width), lambda j, w: (0, j, 0))] * chips
            + [whole((orbitals, depth))],
            scratch_shapes=[pltpu.VMEM((orbitals, depth), BF16)],
        ),
        out_shape=[jax.ShapeDtypeStruct((share, first, width), BF16)] * chips
        + [jax.ShapeDtypeStruct((orbitals, depth), BF16)],
        compiler_params=params(),
        cost_estimate=cost(orbitals * depth * first * width, moved.size * 2),
        name="first_products",
    )(where, own, other, moved)


def rest_kernel(chips, spans, x_ref, table_ref, _, *outs):
    slots, depth, rows, width = x_ref.shape
    block = jnp.swapaxes(x_ref[...].reshape(slots * depth, rows, width), 0, 1)
    value = products(table_ref[...], block)
    share = table_ref.shape[0] // chips
    for (k, lo, hi), out in zip(spans, outs):
        out[...] = value[k * share + lo : k * share + hi]


def rest_products(chips, spans, integrals, table, first, after):
    slots, depth, total, width = integrals.shape
    orbitals = table.shape[0]
    rest = total - first
    skip = first // ROWS
    shapes = [hi - lo for _, lo, hi in spans]
    return pl.pallas_call(
        functools.partial(rest_kernel, chips, spans),
        grid=(rest // ROWS,),
        in_specs=[
            pl.BlockSpec((slots, depth, ROWS, width), lambda j: (0, 0, j + skip, 0)),
            pl.BlockSpec(table.shape, lambda j: (0, 0)),
            pl.BlockSpec(memory_space=pl.ANY),
        ],
        out_specs=[pl.BlockSpec((n, ROWS, width), lambda j: (0, j, 0)) for n in shapes],
        out_shape=[jax.ShapeDtypeStruct((n, rest, width), BF16) for n in shapes],
        compiler_params=params(),
        cost_estimate=cost(orbitals * table.shape[1] * rest * width, integrals.size * 2),
        name="rest_products",
    )(integrals, table, after)


def metric_kernel(where, own_ref, near_ref, far_ref, o_ref):
    aux = where.shape[0] - 1
    width = o_ref.shape[1] // aux
    for kz in range(aux):
        start = pl.multiple_of(where[where[aux] ^ kz] * width, width)
        at = 0
        for ref in (own_ref, near_ref, far_ref):
            size = ref.shape[0]
            o_ref[at : at + size, kz * width : (kz + 1) * width] = ref[:, pl.ds(start, width)]
            at += size


def ordered_metric(where, own, near, far):
    total = own.shape[0] + near.shape[0] + far.shape[0]
    return pl.pallas_call(
        metric_kernel,
        in_specs=[pl.BlockSpec(memory_space=pltpu.SMEM)] + [WHOLE] * 3,
        out_specs=WHOLE,
        out_shape=jax.ShapeDtypeStruct((total, own.shape[1]), BF16),
        compiler_params=params(),
        cost_estimate=cost(0, total * own.shape[1] * 4),
        name="ordered_metric",
    )(where, own, near, far)


def add_group(aux, bas, lo, hi, starts, metric, early, late, total):
    chips = aux * bas
    for i in range(lo, hi):
        columns = []
        for k in range(chips):
            columns.append(jnp.concatenate([early[k][i], late[k][starts[k] + i - lo]], axis=0))
        stacked = jnp.concatenate(
            [jnp.concatenate(columns[kz * bas : (kz + 1) * bas], axis=1) for kz in range(aux)],
            axis=0,
        )
        fitted = jnp.dot(metric, stacked, preferred_element_type=F32).astype(BF16)
        total = total + lax.dot_general(
            fitted, fitted, (((0,), (0,)), ((), ())), preferred_element_type=F32
        )
    return total


def group_kernel(aux, bas, lo, hi, starts, started, last, *refs):
    chips = aux * bas
    refs = list(refs)
    where = refs.pop(0) if last else None
    metric = refs.pop(0)[...]
    early = [refs.pop(0) for _ in range(chips)]
    late = [refs.pop(0) for _ in range(chips)]
    side = bas * late[0].shape[2]
    total = refs.pop(0)[...] if started else jnp.zeros((side, side), F32)
    total = add_group(aux, bas, lo, hi, starts, metric, early, late, total)
    if not last:
        refs[0][...] = total
        return
    kept, near, away, scratch = refs
    scratch[...] = total
    width = side // bas
    piece = kept.shape[1]
    for ka in range(aux):
        a = where[0] ^ ka
        for who in range(2):
            row = (a * 2 + (where[2] ^ who)) * piece
            block = lax.div(row, width) ^ where[1]
            start = pl.multiple_of(block * width + lax.rem(row, width), piece)
            value = scratch[pl.ds(start, piece), :]
            if who:
                away[ka] = value
            else:
                kept[ka] = value[:, :width]
                near[ka] = value[:, width:]


def group(aux, bas, lo, hi, metric, early, late, total, where=None):
    starts = tuple(start for _, start in late)
    late = [value for value, _ in late]
    last, started = where is not None, total is not None
    width = late[0].shape[2]
    side = bas * width
    args = ([where] if last else []) + [metric, *early, *late] + ([total] if started else [])
    specs = [WHOLE] * len(args)
    if last:
        specs[0] = pl.BlockSpec(memory_space=pltpu.SMEM)
        piece = side // (aux * 2)
        out = [
            jax.ShapeDtypeStruct((aux, piece, width), F32),
            jax.ShapeDtypeStruct((aux, piece, width), F32),
            jax.ShapeDtypeStruct((aux, piece, side), F32),
        ]
    else:
        out = jax.ShapeDtypeStruct((side, side), F32)
    rows = metric.shape[0]
    macs = (hi - lo) * (rows * rows * side + rows * side * side)
    return pl.pallas_call(
        functools.partial(group_kernel, aux, bas, lo, hi, starts, started, last),
        in_specs=specs,
        out_specs=[WHOLE] * 3 if last else WHOLE,
        out_shape=out,
        scratch_shapes=[pltpu.VMEM((side, side), F32)] if last else [],
        compiler_params=params(),
        cost_estimate=cost(macs, (hi - lo) * rows * side * 2),
        name="group",
    )(*args)


def per_device(integrals, screening, coefficients, metric, aux_owner):
    aux = lax.axis_size("aux")
    bas = lax.axis_size("bas")
    chips = aux * bas
    integrals = integrals[0, 0]
    orbitals = coefficients.shape[1]
    share = orbitals // chips
    a, b, o = (lax.axis_index(name) for name in ("aux", "bas", "occ"))
    first = integrals.shape[2] // 4
    groups = ((0, 6), (6, 12), (12, share))
    inner, outer = (1, 2, 3), (4, 5, 6, 7)

    def swap(value, kz=0, kx=0):
        pairs = [
            (i * bas + j, (i ^ kz) * bas + (j ^ kx)) for i in range(aux) for j in range(bas)
        ]
        return lax.ppermute(value, ("aux", "bas"), pairs)

    def across(value):
        return lax.ppermute(value, "occ", [(0, 1), (1, 0)])

    def after(value, *earlier):
        return lax.optimization_barrier((value, *earlier))[0]

    integrals = pltpu.with_memory_space_constraint(integrals, pltpu.HBM)
    other = swap(coefficients, kx=1)
    moved = relayout(integrals, first)

    rows = metric.shape[0] // 4
    part = lax.dynamic_slice_in_dim(after(metric, moved), (b * 2 + o) * rows, rows, axis=0)
    pieces = [swap(part, kz=kz) for kz in range(1, aux)]
    where = jnp.concatenate([jnp.stack([a * bas + b, b]), screening[0, 0]]).astype(jnp.int32)
    *early, table = first_products(
        chips, where, after(coefficients, *pieces), other, moved, first
    )

    sent = []

    def send(k, value):
        if len(sent) >= WINDOW:
            value = after(value, sent[-WINDOW])
        sent.append(swap(value, k // bas, k % bas))
        return sent[-1]

    spans = [(k, lo, hi) for lo, hi in groups for k in outer]
    spans += [(k, 0, share) for k in (0, *inner)]
    got = {k: send(k, early[k]) for k in (4, 5, 1, 6, 7)}
    late = rest_products(chips, tuple(spans), integrals, table, first, got[1])
    for k in (2, 3):
        got[k] = send(k, after(early[k], late[0]))
    got[0] = early[0]
    made = dict(zip(spans, late))
    here = {(0, 0, share): made[0, 0, share]}
    for g, (lo, hi) in enumerate(groups):
        for at, k in enumerate(outer):
            here[k, lo, hi] = send(k, made[k, lo, hi])
            if g == 0 and at:
                here[at, 0, share] = send(at, made[at, 0, share])

    near = jnp.concatenate(pieces, axis=0)
    near = jnp.concatenate([near, swap(near, kx=1)], axis=0)
    far = across(near)
    ordered = ordered_metric(
        jnp.concatenate([aux_owner, a[None]]).astype(jnp.int32), metric, near, far
    )
    early = [got[k] for k in range(chips)]
    total = None
    for g, (lo, hi) in enumerate(groups):
        part = [(here[k, 0, share], lo) if k < 4 else (here[k, lo, hi], 0) for k in range(chips)]
        place = jnp.stack([a, b, o]).astype(jnp.int32) if g == len(groups) - 1 else None
        total = group(aux, bas, lo, hi, ordered, early, part, total, place)
    kept, near, away = total
    away = across(away)
    width = kept.shape[2]
    kept = kept + away[:, :, :width]
    near = near + away[:, :, width:]
    kept = kept + swap(near, kx=1)
    value = kept[0]
    for kz in range(1, aux):
        value = value + swap(kept[kz], kz=kz)
    return value.T


def plain_device(integrals, screening, coefficients, metric, aux_owner):
    block_size = integrals.shape[-1]
    aux_count = lax.axis_size("aux")
    bas_count = lax.axis_size("bas")
    occ_count = lax.axis_size("occ")
    gathered = lax.all_gather(coefficients, "bas", axis=0, tiled=True)
    orbitals = gathered.shape[1]
    by_block = gathered.reshape(gathered.shape[0] // block_size, block_size, orbitals)
    picked = jnp.take(by_block, screening[0, 0], axis=0)
    stacked = integrals[0, 0].reshape(integrals.shape[2], block_size, block_size * block_size)
    contracted = lax.dot_general(
        picked, stacked, (((0, 1), (0, 1)), ((), ())), preferred_element_type=jnp.float32
    )
    transformed = contracted.astype(jnp.bfloat16)
    share = orbitals // (aux_count * bas_count)
    moved = lax.all_to_all(
        transformed.reshape(orbitals, 1, block_size, block_size),
        ("aux", "bas"),
        split_axis=0,
        concat_axis=1,
        tiled=True,
    )
    moved = moved.reshape(share, aux_count, bas_count, block_size, block_size)
    aux_table = (aux_owner[:, None] == jnp.arange(aux_count, dtype=jnp.int32)[None, :]).astype(
        jnp.bfloat16
    )
    piece = lax.all_gather(metric, "aux", axis=0, tiled=True)
    columns = piece.reshape(piece.shape[0], aux_count, block_size)
    ordered = jnp.einsum(
        "rgp,ag->rap", columns, aux_table, preferred_element_type=jnp.float32
    ).astype(jnp.bfloat16)
    fitted = jnp.einsum(
        "rap,iabpm->irbm", ordered, moved, preferred_element_type=jnp.float32
    ).astype(jnp.bfloat16)
    partial_value = jnp.einsum(
        "iqbm,iqcn->bmcn", fitted, fitted, preferred_element_type=jnp.float32
    )
    column_share = bas_count * block_size // (aux_count * occ_count)
    arranged = partial_value.reshape(bas_count, block_size, aux_count, occ_count, column_share)
    arranged = arranged.transpose(2, 0, 3, 1, 4).reshape(-1, column_share)
    return lax.psum_scatter(arranged, ("aux", "bas", "occ"), scatter_dimension=0, tiled=True)


def solution(mesh):
    in_specs = (
        P(("parts", "aux"), "bas", None, None, None, None),
        P(("parts", "aux"), "bas", None),
        P(("parts", "bas"), "occ"),
        P(("parts", "aux"), None),
        P("parts"),
    )
    out_specs = P(("parts", "bas"), ("aux", "occ"))
    small = mesh.shape["aux"] == 4 and mesh.shape["bas"] == 2 and mesh.shape["occ"] == 2
    return jax.shard_map(
        per_device if small else plain_device,
        mesh=mesh,
        in_specs=in_specs,
        out_specs=out_specs,
        check_vma=False,
    )
```

```python
import functools

import jax
import jax.numpy as jnp
from jax import lax
from jax.experimental import pallas as pl
from jax.experimental.pallas import tpu as pltpu
from jax.sharding import PartitionSpec as P

F32 = jnp.float32
BF16 = jnp.bfloat16
ROWS = 16
WINDOW = 5
GROUPS = ((0, 7), (7, 13), (13, 16))
FIRST = 32
OPEN = (4, 1, 5, 3, 6, 7)
ORDER = ((2, -1), (4, 0), (5, 0), (1, 0), (6, 0), (2, 0), (7, 0), (3, 0), (4, 1), (5, 1), (7, 1), (6, 1), (4, 2), (5, 2), (6, 2), (7, 2))
RESTDEP = 1
LAST = (2, 3, 1)
WHOLE = pl.BlockSpec(memory_space=pltpu.VMEM)


def params(mib=40):
    return pltpu.CompilerParams(vmem_limit_bytes=mib * 2**20)


def cost(macs, size):
    return pl.CostEstimate(flops=2 * macs, bytes_accessed=size, transcendentals=0)


def relayout_kernel(x_ref, o_ref):
    slots, depth, rows, width = x_ref.shape
    o_ref[...] = jnp.swapaxes(x_ref[...].reshape(slots * depth, rows, width), 0, 1)


def relayout(integrals, first):
    slots, depth, _, width = integrals.shape
    return pl.pallas_call(
        relayout_kernel,
        grid=(first // ROWS,),
        in_specs=[pl.BlockSpec((slots, depth, ROWS, width), lambda j: (0, 0, j, 0))],
        out_specs=pl.BlockSpec((ROWS, slots * depth, width), lambda j: (j, 0, 0)),
        out_shape=jax.ShapeDtypeStruct((first, slots * depth, width), BF16),
        compiler_params=params(),
        cost_estimate=cost(0, 2 * first * slots * depth * width * 2),
        name="relayout",
    )(integrals)


def products(table, block):
    parts = []
    for p in range(0, block.shape[0], 2):
        pair = jnp.concatenate([block[p], block[p + 1]], axis=1)
        value = jnp.dot(table, pair, preferred_element_type=F32).astype(BF16)
        width = block.shape[2]
        parts += [value[:, :width], value[:, width:]]
    return jnp.swapaxes(jnp.stack(parts), 0, 1)


def first_kernel(chips, where, own_ref, other_ref, x_ref, *rest):
    outs, table_ref, plain = rest[:chips], rest[chips], rest[chips + 1]
    share = table_ref.shape[0] // chips

    @pl.when(pl.program_id(0) == 0)
    def _():
        block = plain.shape[0]
        held = own_ref.shape[0] // block
        for s in range(plain.shape[1] // block):
            name = where[2 + s]
            away = lax.div(name, held) != where[1]
            start = pl.multiple_of(lax.rem(name, held) * block, block)
            mine = own_ref[pl.ds(start, block), :].astype(F32)
            theirs = other_ref[pl.ds(start, block), :].astype(F32)
            picked = jnp.where(away, theirs, mine)
            plain[:, s * block : (s + 1) * block] = picked.T.astype(BF16)
        for k in range(chips):
            start = pl.multiple_of((where[0] ^ k) * share, share)
            table_ref[k * share : (k + 1) * share, :] = plain[pl.ds(start, share), :]

    value = products(table_ref[...], x_ref[...])
    for k in range(chips):
        outs[k][...] = value[k * share : (k + 1) * share]


def first_products(chips, where, own, other, moved, first):
    _, depth, width = moved.shape
    orbitals = own.shape[1]
    share = orbitals // chips
    whole = lambda shape: pl.BlockSpec(shape, lambda j, w: (0,) * len(shape))
    return pl.pallas_call(
        functools.partial(first_kernel, chips),
        grid_spec=pltpu.PrefetchScalarGridSpec(
            num_scalar_prefetch=1,
            grid=(first // ROWS,),
            in_specs=[
                whole(own.shape),
                whole(other.shape),
                pl.BlockSpec((ROWS, depth, width), lambda j, w: (j, 0, 0)),
            ],
            out_specs=[pl.BlockSpec((share, ROWS, width), lambda j, w: (0, j, 0))] * chips
            + [whole((orbitals, depth))],
            scratch_shapes=[pltpu.VMEM((orbitals, depth), BF16)],
        ),
        out_shape=[jax.ShapeDtypeStruct((share, first, width), BF16)] * chips
        + [jax.ShapeDtypeStruct((orbitals, depth), BF16)],
        compiler_params=params(),
        cost_estimate=cost(orbitals * depth * first * width, moved.size * 2),
        name="first_products",
    )(where, own, other, moved)


def rest_kernel(chips, spans, x_ref, table_ref, _, *outs):
    slots, depth, rows, width = x_ref.shape
    block = jnp.swapaxes(x_ref[...].reshape(slots * depth, rows, width), 0, 1)
    value = products(table_ref[...], block)
    share = table_ref.shape[0] // chips
    for (k, lo, hi), out in zip(spans, outs):
        out[...] = value[k * share + lo : k * share + hi]


def rest_products(chips, spans, integrals, table, first, after):
    slots, depth, total, width = integrals.shape
    orbitals = table.shape[0]
    rest = total - first
    skip = first // ROWS
    shapes = [hi - lo for _, lo, hi in spans]
    return pl.pallas_call(
        functools.partial(rest_kernel, chips, spans),
        grid=(rest // ROWS,),
        in_specs=[
            pl.BlockSpec((slots, depth, ROWS, width), lambda j: (0, 0, j + skip, 0)),
            pl.BlockSpec(table.shape, lambda j: (0, 0)),
            pl.BlockSpec(memory_space=pl.ANY),
        ],
        out_specs=[pl.BlockSpec((n, ROWS, width), lambda j: (0, j, 0)) for n in shapes],
        out_shape=[jax.ShapeDtypeStruct((n, rest, width), BF16) for n in shapes],
        compiler_params=params(),
        cost_estimate=cost(orbitals * table.shape[1] * rest * width, integrals.size * 2),
        name="rest_products",
    )(integrals, table, after)


def metric_kernel(where, *refs):
    o_ref = refs[-1]
    aux = where.shape[0] - 1
    width = o_ref.shape[1] // aux
    for kz in range(aux):
        start = pl.multiple_of(where[where[aux] ^ kz] * width, width)
        at = 0
        for ref in refs[:-1]:
            size = ref.shape[0]
            o_ref[at : at + size, kz * width : (kz + 1) * width] = ref[:, pl.ds(start, width)]
            at += size


def ordered_metric(where, pieces):
    total = sum(piece.shape[0] for piece in pieces)
    columns = pieces[0].shape[1]
    return pl.pallas_call(
        metric_kernel,
        in_specs=[pl.BlockSpec(memory_space=pltpu.SMEM)] + [WHOLE] * len(pieces),
        out_specs=WHOLE,
        out_shape=jax.ShapeDtypeStruct((total, columns), BF16),
        compiler_params=params(),
        cost_estimate=cost(0, total * columns * 4),
        name="ordered_metric",
    )(where, *pieces)


def add_group(aux, bas, lo, hi, starts, metric, early, late, total):
    chips = aux * bas
    fitted = []
    for i in range(lo, hi):
        columns = []
        for k in range(chips):
            columns.append(jnp.concatenate([early[k][i], late[k][starts[k] + i - lo]], axis=0))
        stacked = jnp.concatenate(
            [jnp.concatenate(columns[kz * bas : (kz + 1) * bas], axis=1) for kz in range(aux)],
            axis=0,
        )
        fitted.append(jnp.dot(metric, stacked, preferred_element_type=F32).astype(BF16))
    fitted = jnp.concatenate(fitted, axis=0)
    return total + lax.dot_general(
        fitted, fitted, (((0,), (0,)), ((), ())), preferred_element_type=F32
    )


def group_kernel(aux, bas, lo, hi, starts, started, last, *refs):
    chips = aux * bas
    refs = list(refs)
    where = refs.pop(0) if last else None
    metric = refs.pop(0)[...]
    early = [refs.pop(0) for _ in range(chips)]
    late = [refs.pop(0) for _ in range(chips)]
    side = bas * late[0].shape[2]
    total = refs.pop(0)[...] if started else jnp.zeros((side, side), F32)
    total = add_group(aux, bas, lo, hi, starts, metric, early, late, total)
    if not last:
        refs[0][...] = total
        return
    kept, near, away, scratch = refs
    scratch[...] = total
    width = side // bas
    piece = kept.shape[1]
    for ka in range(aux):
        a = where[0] ^ ka
        for who in range(2):
            row = (a * 2 + (where[2] ^ who)) * piece
            block = lax.div(row, width) ^ where[1]
            start = pl.multiple_of(block * width + lax.rem(row, width), piece)
            value = scratch[pl.ds(start, piece), :]
            if who:
                away[ka] = value
            else:
                kept[ka] = value[:, :width]
                near[ka] = value[:, width:]


def group(aux, bas, lo, hi, metric, early, late, total, where=None):
    starts = tuple(start for _, start in late)
    late = [value for value, _ in late]
    last, started = where is not None, total is not None
    width = late[0].shape[2]
    side = bas * width
    args = ([where] if last else []) + [metric, *early, *late] + ([total] if started else [])
    specs = [WHOLE] * len(args)
    if last:
        specs[0] = pl.BlockSpec(memory_space=pltpu.SMEM)
        piece = side // (aux * 2)
        out = [
            jax.ShapeDtypeStruct((aux, piece, width), F32),
            jax.ShapeDtypeStruct((aux, piece, width), F32),
            jax.ShapeDtypeStruct((aux, piece, side), F32),
        ]
    else:
        out = jax.ShapeDtypeStruct((side, side), F32)
    rows = metric.shape[0]
    macs = (hi - lo) * (rows * rows * side + rows * side * side)
    return pl.pallas_call(
        functools.partial(group_kernel, aux, bas, lo, hi, starts, started, last),
        in_specs=specs,
        out_specs=[WHOLE] * 3 if last else WHOLE,
        out_shape=out,
        scratch_shapes=[pltpu.VMEM((side, side), F32)] if last else [],
        compiler_params=params(),
        cost_estimate=cost(macs, (hi - lo) * rows * side * 2),
        name="group",
    )(*args)


def per_device(integrals, screening, coefficients, metric, aux_owner):
    aux = lax.axis_size("aux")
    bas = lax.axis_size("bas")
    chips = aux * bas
    integrals = integrals[0, 0]
    orbitals = coefficients.shape[1]
    share = orbitals // chips
    a, b, o = (lax.axis_index(name) for name in ("aux", "bas", "occ"))
    first = FIRST
    groups = GROUPS
    inner, outer = (1, 2, 3), (4, 5, 6, 7)

    def swap(value, kz=0, kx=0):
        pairs = [
            (i * bas + j, (i ^ kz) * bas + (j ^ kx)) for i in range(aux) for j in range(bas)
        ]
        return lax.ppermute(value, ("aux", "bas"), pairs)

    def across(value):
        return lax.ppermute(value, "occ", [(0, 1), (1, 0)])

    def after(value, *earlier):
        return lax.optimization_barrier((value, *earlier))[0]

    integrals = pltpu.with_memory_space_constraint(integrals, pltpu.HBM)
    other = swap(coefficients, kx=1)
    moved = relayout(integrals, first)
    where = jnp.concatenate([jnp.stack([a * bas + b, b]), screening[0, 0]]).astype(jnp.int32)
    rows = metric.shape[0] // 4
    held = lax.dynamic_slice_in_dim(metric, (b * 2 + o) * rows, rows, axis=0)
    held = [held, swap(held, kz=2)]
    *early, table = first_products(
        chips, where, after(coefficients, *held), other, moved, first
    )
    held = jnp.concatenate(held, axis=0)
    sent = []

    def send(value, kz, kx):
        if len(sent) >= WINDOW:
            value = after(value, sent[-WINDOW])
        sent.append(swap(value, kz, kx))
        return sent[-1]

    got = {(k, -1): send(early[k], k // bas, k % bas) for k in OPEN}
    got[0, -1] = early[0]
    spans = [(k, lo, hi) for lo, hi in groups for k in outer]
    spans += [(k, 0, share) for k in (0, *inner)]
    late = rest_products(chips, tuple(spans), integrals, table, first, got[RESTDEP, -1])
    made = dict(zip(spans, late))
    got[0, 0] = made[0, 0, share]
    for k, g in ORDER:
        if g < 0:
            value = after(early[k], late[0])
        else:
            value = made[(k, *groups[g])] if k in outer else made[k, 0, share]
        got[k, g] = send(value, k // bas, k % bas)
    held = jnp.concatenate([held, swap(held, kz=1)], axis=0)
    held = jnp.concatenate([held, swap(held, kx=1)], axis=0)
    ordered = ordered_metric(
        jnp.concatenate([aux_owner, a[None]]).astype(jnp.int32), [held, across(held)]
    )
    early = [got[k, -1] for k in range(chips)]
    total = None
    for g, (lo, hi) in enumerate(groups):
        part = [
            (got[k, g], 0) if k in outer else (got[k, 0], lo) for k in range(chips)
        ]
        place = jnp.stack([a, b, o]).astype(jnp.int32) if g == len(groups) - 1 else None
        total = group(aux, bas, lo, hi, ordered, early, part, total, place)
    kept, near, away = total
    away = across(away)
    width = kept.shape[2]
    kept = kept + away[:, :, :width]
    near = near + away[:, :, width:]
    kept = kept + swap(near, kx=1)
    value = kept[0]
    for kz in LAST:
        value = value + swap(kept[kz], kz=kz)
    return value.T


def plain_device(integrals, screening, coefficients, metric, aux_owner):
    block_size = integrals.shape[-1]
    aux_count = lax.axis_size("aux")
    bas_count = lax.axis_size("bas")
    occ_count = lax.axis_size("occ")
    gathered = lax.all_gather(coefficients, "bas", axis=0, tiled=True)
    orbitals = gathered.shape[1]
    by_block = gathered.reshape(gathered.shape[0] // block_size, block_size, orbitals)
    picked = jnp.take(by_block, screening[0, 0], axis=0)
    stacked = integrals[0, 0].reshape(integrals.shape[2], block_size, block_size * block_size)
    contracted = lax.dot_general(
        picked, stacked, (((0, 1), (0, 1)), ((), ())), preferred_element_type=jnp.float32
    )
    transformed = contracted.astype(jnp.bfloat16)
    share = orbitals // (aux_count * bas_count)
    moved = lax.all_to_all(
        transformed.reshape(orbitals, 1, block_size, block_size),
        ("aux", "bas"),
        split_axis=0,
        concat_axis=1,
        tiled=True,
    )
    moved = moved.reshape(share, aux_count, bas_count, block_size, block_size)
    aux_table = (aux_owner[:, None] == jnp.arange(aux_count, dtype=jnp.int32)[None, :]).astype(
        jnp.bfloat16
    )
    piece = lax.all_gather(metric, "aux", axis=0, tiled=True)
    columns = piece.reshape(piece.shape[0], aux_count, block_size)
    ordered = jnp.einsum(
        "rgp,ag->rap", columns, aux_table, preferred_element_type=jnp.float32
    ).astype(jnp.bfloat16)
    fitted = jnp.einsum(
        "rap,iabpm->irbm", ordered, moved, preferred_element_type=jnp.float32
    ).astype(jnp.bfloat16)
    partial_value = jnp.einsum(
        "iqbm,iqcn->bmcn", fitted, fitted, preferred_element_type=jnp.float32
    )
    column_share = bas_count * block_size // (aux_count * occ_count)
    arranged = partial_value.reshape(bas_count, block_size, aux_count, occ_count, column_share)
    arranged = arranged.transpose(2, 0, 3, 1, 4).reshape(-1, column_share)
    return lax.psum_scatter(arranged, ("aux", "bas", "occ"), scatter_dimension=0, tiled=True)


def solution(mesh):
    in_specs = (
        P(("parts", "aux"), "bas", None, None, None, None),
        P(("parts", "aux"), "bas", None),
        P(("parts", "bas"), "occ"),
        P(("parts", "aux"), None),
        P("parts"),
    )
    out_specs = P(("parts", "bas"), ("aux", "occ"))
    small = mesh.shape["aux"] == 4 and mesh.shape["bas"] == 2 and mesh.shape["occ"] == 2
    return jax.shard_map(
        per_device if small else plain_device,
        mesh=mesh,
        in_specs=in_specs,
        out_specs=out_specs,
        check_vma=False,
    )
```

```python
import functools

import jax
import jax.numpy as jnp
from jax import lax
from jax.experimental import pallas as pl
from jax.experimental.pallas import tpu as pltpu
from jax.sharding import PartitionSpec as P

F32 = jnp.float32
BF16 = jnp.bfloat16
ROWS = 16
WINDOW = 5
GROUPS = ((0, 7), (7, 13), (13, 16))
FIRST = 32
OPEN = (4, 1, 5, 3, 6, 7)
ORDER = (
    ((2, -1), (4, 0), (5, 0), (1, 0), (6, 0), (2, 0), (7, 0), (3, 0))
    + ((4, 1), (5, 1), (7, 1), (6, 1))
    + ((7, 2), (4, 2), (5, 2), (6, 2))
)
RESTDEP = 1
LAST = (3, 2, 1)
WHOLE = pl.BlockSpec(memory_space=pltpu.VMEM)


def params(mib=40):
    return pltpu.CompilerParams(vmem_limit_bytes=mib * 2**20)


def cost(macs, size):
    return pl.CostEstimate(flops=2 * macs, bytes_accessed=size, transcendentals=0)


def relayout_kernel(x_ref, o_ref):
    slots, depth, rows, width = x_ref.shape
    o_ref[...] = jnp.swapaxes(x_ref[...].reshape(slots * depth, rows, width), 0, 1)


def relayout(integrals, first):
    slots, depth, _, width = integrals.shape
    return pl.pallas_call(
        relayout_kernel,
        grid=(first // ROWS,),
        in_specs=[pl.BlockSpec((slots, depth, ROWS, width), lambda j: (0, 0, j, 0))],
        out_specs=pl.BlockSpec((ROWS, slots * depth, width), lambda j: (j, 0, 0)),
        out_shape=jax.ShapeDtypeStruct((first, slots * depth, width), BF16),
        compiler_params=params(),
        cost_estimate=cost(0, 2 * first * slots * depth * width * 2),
        name="relayout",
    )(integrals)


def products(table, block):
    parts = []
    for p in range(0, block.shape[0], 2):
        pair = jnp.concatenate([block[p], block[p + 1]], axis=1)
        value = jnp.dot(table, pair, preferred_element_type=F32).astype(BF16)
        width = block.shape[2]
        parts += [value[:, :width], value[:, width:]]
    return jnp.swapaxes(jnp.stack(parts), 0, 1)


def first_kernel(chips, where, own_ref, other_ref, x_ref, *rest):
    outs, table_ref, plain = rest[:chips], rest[chips], rest[chips + 1]
    share = table_ref.shape[0] // chips
    block = plain.shape[0]
    held = own_ref.shape[0] // block
    for s in range(plain.shape[1] // block):
        name = where[2 + s]
        away = lax.div(name, held) != where[1]
        start = pl.multiple_of(lax.rem(name, held) * block, block)
        mine = own_ref[pl.ds(start, block), :].astype(F32)
        theirs = other_ref[pl.ds(start, block), :].astype(F32)
        picked = jnp.where(away, theirs, mine)
        plain[:, s * block : (s + 1) * block] = picked.T.astype(BF16)
    for k in range(chips):
        start = pl.multiple_of((where[0] ^ k) * share, share)
        table_ref[k * share : (k + 1) * share, :] = plain[pl.ds(start, share), :]
    for at in range(0, x_ref.shape[0], ROWS):
        value = products(table_ref[...], x_ref[at : at + ROWS])
        for k in range(chips):
            outs[k][:, at : at + ROWS, :] = value[k * share : (k + 1) * share]


def first_products(chips, where, own, other, moved, first):
    _, depth, width = moved.shape
    orbitals = own.shape[1]
    share = orbitals // chips
    return pl.pallas_call(
        functools.partial(first_kernel, chips),
        in_specs=[pl.BlockSpec(memory_space=pltpu.SMEM)] + [WHOLE] * 3,
        out_specs=[WHOLE] * (chips + 1),
        out_shape=[jax.ShapeDtypeStruct((share, first, width), BF16)] * chips
        + [jax.ShapeDtypeStruct((orbitals, depth), BF16)],
        scratch_shapes=[pltpu.VMEM((orbitals, depth), BF16)],
        compiler_params=params(),
        cost_estimate=cost(orbitals * depth * first * width, moved.size * 2),
        name="first_products",
    )(where, own, other, moved)


def rest_kernel(chips, spans, x_ref, table_ref, _, *outs):
    slots, depth, rows, width = x_ref.shape
    block = jnp.swapaxes(x_ref[...].reshape(slots * depth, rows, width), 0, 1)
    value = products(table_ref[...], block)
    share = table_ref.shape[0] // chips
    for (k, lo, hi), out in zip(spans, outs):
        out[...] = value[k * share + lo : k * share + hi]


def rest_products(chips, spans, integrals, table, first, after):
    slots, depth, total, width = integrals.shape
    orbitals = table.shape[0]
    rest = total - first
    skip = first // ROWS
    shapes = [hi - lo for _, lo, hi in spans]
    return pl.pallas_call(
        functools.partial(rest_kernel, chips, spans),
        grid=(rest // ROWS,),
        in_specs=[
            pl.BlockSpec((slots, depth, ROWS, width), lambda j: (0, 0, j + skip, 0)),
            pl.BlockSpec(table.shape, lambda j: (0, 0)),
            pl.BlockSpec(memory_space=pl.ANY),
        ],
        out_specs=[pl.BlockSpec((n, ROWS, width), lambda j: (0, j, 0)) for n in shapes],
        out_shape=[jax.ShapeDtypeStruct((n, rest, width), BF16) for n in shapes],
        compiler_params=params(),
        cost_estimate=cost(orbitals * table.shape[1] * rest * width, integrals.size * 2),
        name="rest_products",
    )(integrals, table, after)


def metric_kernel(where, *refs):
    o_ref = refs[-1]
    aux = where.shape[0] - 1
    width = o_ref.shape[1] // aux
    for kz in range(aux):
        start = pl.multiple_of(where[where[aux] ^ kz] * width, width)
        at = 0
        for ref in refs[:-1]:
            size = ref.shape[0]
            o_ref[at : at + size, kz * width : (kz + 1) * width] = ref[:, pl.ds(start, width)]
            at += size


def ordered_metric(where, pieces):
    total = sum(piece.shape[0] for piece in pieces)
    columns = pieces[0].shape[1]
    return pl.pallas_call(
        metric_kernel,
        in_specs=[pl.BlockSpec(memory_space=pltpu.SMEM)] + [WHOLE] * len(pieces),
        out_specs=WHOLE,
        out_shape=jax.ShapeDtypeStruct((total, columns), BF16),
        compiler_params=params(),
        cost_estimate=cost(0, total * columns * 4),
        name="ordered_metric",
    )(where, *pieces)


def add_group(aux, bas, lo, hi, starts, metric, early, late, total):
    chips = aux * bas
    fitted = []
    for i in range(lo, hi):
        columns = []
        for k in range(chips):
            columns.append(jnp.concatenate([early[k][i], late[k][starts[k] + i - lo]], axis=0))
        stacked = jnp.concatenate(
            [jnp.concatenate(columns[kz * bas : (kz + 1) * bas], axis=1) for kz in range(aux)],
            axis=0,
        )
        fitted.append(jnp.dot(metric, stacked, preferred_element_type=F32).astype(BF16))
    fitted = jnp.concatenate(fitted, axis=0)
    return total + lax.dot_general(
        fitted, fitted, (((0,), (0,)), ((), ())), preferred_element_type=F32
    )


def group_kernel(aux, bas, lo, hi, starts, started, last, *refs):
    chips = aux * bas
    refs = list(refs)
    where = refs.pop(0) if last else None
    metric = refs.pop(0)[...]
    early = [refs.pop(0) for _ in range(chips)]
    late = [refs.pop(0) for _ in range(chips)]
    side = bas * late[0].shape[2]
    total = refs.pop(0)[...] if started else jnp.zeros((side, side), F32)
    total = add_group(aux, bas, lo, hi, starts, metric, early, late, total)
    if not last:
        refs[0][...] = total
        return
    kept, near, away, scratch = refs
    scratch[...] = total
    width = side // bas
    piece = kept.shape[1]
    for ka in range(aux):
        a = where[0] ^ ka
        for who in range(2):
            row = (a * 2 + (where[2] ^ who)) * piece
            block = lax.div(row, width) ^ where[1]
            start = pl.multiple_of(block * width + lax.rem(row, width), piece)
            value = scratch[pl.ds(start, piece), :]
            if who:
                away[ka] = value
            else:
                kept[ka] = value[:, :width]
                near[ka] = value[:, width:]


def group(aux, bas, lo, hi, metric, early, late, total, where=None):
    starts = tuple(start for _, start in late)
    late = [value for value, _ in late]
    last, started = where is not None, total is not None
    width = late[0].shape[2]
    side = bas * width
    args = ([where] if last else []) + [metric, *early, *late] + ([total] if started else [])
    specs = [WHOLE] * len(args)
    if last:
        specs[0] = pl.BlockSpec(memory_space=pltpu.SMEM)
        piece = side // (aux * 2)
        out = [
            jax.ShapeDtypeStruct((aux, piece, width), F32),
            jax.ShapeDtypeStruct((aux, piece, width), F32),
            jax.ShapeDtypeStruct((aux, piece, side), F32),
        ]
    else:
        out = jax.ShapeDtypeStruct((side, side), F32)
    rows = metric.shape[0]
    macs = (hi - lo) * (rows * rows * side + rows * side * side)
    return pl.pallas_call(
        functools.partial(group_kernel, aux, bas, lo, hi, starts, started, last),
        in_specs=specs,
        out_specs=[WHOLE] * 3 if last else WHOLE,
        out_shape=out,
        scratch_shapes=[pltpu.VMEM((side, side), F32)] if last else [],
        compiler_params=params(),
        cost_estimate=cost(macs, (hi - lo) * rows * side * 2),
        name="group",
    )(*args)


def per_device(integrals, screening, coefficients, metric, aux_owner):
    aux = lax.axis_size("aux")
    bas = lax.axis_size("bas")
    chips = aux * bas
    integrals = integrals[0, 0]
    orbitals = coefficients.shape[1]
    share = orbitals // chips
    a, b, o = (lax.axis_index(name) for name in ("aux", "bas", "occ"))
    first = FIRST
    groups = GROUPS
    inner, outer = (1, 2, 3), (4, 5, 6, 7)

    def swap(value, kz=0, kx=0):
        pairs = [
            (i * bas + j, (i ^ kz) * bas + (j ^ kx)) for i in range(aux) for j in range(bas)
        ]
        return lax.ppermute(value, ("aux", "bas"), pairs)

    def across(value):
        return lax.ppermute(value, "occ", [(0, 1), (1, 0)])

    def after(value, *earlier):
        return lax.optimization_barrier((value, *earlier))[0]

    integrals = pltpu.with_memory_space_constraint(integrals, pltpu.HBM)
    other = swap(coefficients, kx=1)
    moved = relayout(integrals, first)
    where = jnp.concatenate([jnp.stack([a * bas + b, b]), screening[0, 0]]).astype(jnp.int32)
    rows = metric.shape[0] // 4
    held = lax.dynamic_slice_in_dim(metric, (b * 2 + o) * rows, rows, axis=0)
    held = [held, swap(held, kz=2)]
    *early, table = first_products(
        chips, where, after(coefficients, *held), other, moved, first
    )
    held = jnp.concatenate(held, axis=0)
    sent = []

    def send(value, kz, kx):
        if len(sent) >= WINDOW:
            value = after(value, sent[-WINDOW])
        sent.append(swap(value, kz, kx))
        return sent[-1]

    got = {(k, -1): send(early[k], k // bas, k % bas) for k in OPEN}
    got[0, -1] = early[0]
    spans = [(k, lo, hi) for lo, hi in groups for k in outer]
    spans += [(k, 0, share) for k in (0, *inner)]
    late = rest_products(chips, tuple(spans), integrals, table, first, got[RESTDEP, -1])
    made = dict(zip(spans, late))
    got[0, 0] = made[0, 0, share]
    for k, g in ORDER:
        if g < 0:
            value = after(early[k], late[0])
        else:
            value = made[(k, *groups[g])] if k in outer else made[k, 0, share]
        got[k, g] = send(value, k // bas, k % bas)
    held = jnp.concatenate([held, swap(held, kz=1)], axis=0)
    held = jnp.concatenate([held, swap(held, kx=1)], axis=0)
    ordered = ordered_metric(
        jnp.concatenate([aux_owner, a[None]]).astype(jnp.int32), [held, across(held)]
    )
    early = [got[k, -1] for k in range(chips)]
    total = None
    for g, (lo, hi) in enumerate(groups):
        part = [
            (got[k, g], 0) if k in outer else (got[k, 0], lo) for k in range(chips)
        ]
        place = jnp.stack([a, b, o]).astype(jnp.int32) if g == len(groups) - 1 else None
        total = group(aux, bas, lo, hi, ordered, early, part, total, place)
    kept, near, away = total
    away = across(away)
    width = kept.shape[2]
    kept = kept + away[:, :, :width]
    near = near + away[:, :, width:]
    kept = kept + swap(near, kx=1)
    value = kept[0]
    for kz in LAST:
        value = value + swap(kept[kz], kz=kz)
    return value.T


def plain_device(integrals, screening, coefficients, metric, aux_owner):
    block_size = integrals.shape[-1]
    aux_count = lax.axis_size("aux")
    bas_count = lax.axis_size("bas")
    occ_count = lax.axis_size("occ")
    gathered = lax.all_gather(coefficients, "bas", axis=0, tiled=True)
    orbitals = gathered.shape[1]
    by_block = gathered.reshape(gathered.shape[0] // block_size, block_size, orbitals)
    picked = jnp.take(by_block, screening[0, 0], axis=0)
    stacked = integrals[0, 0].reshape(integrals.shape[2], block_size, block_size * block_size)
    contracted = lax.dot_general(
        picked, stacked, (((0, 1), (0, 1)), ((), ())), preferred_element_type=jnp.float32
    )
    transformed = contracted.astype(jnp.bfloat16)
    share = orbitals // (aux_count * bas_count)
    moved = lax.all_to_all(
        transformed.reshape(orbitals, 1, block_size, block_size),
        ("aux", "bas"),
        split_axis=0,
        concat_axis=1,
        tiled=True,
    )
    moved = moved.reshape(share, aux_count, bas_count, block_size, block_size)
    aux_table = (aux_owner[:, None] == jnp.arange(aux_count, dtype=jnp.int32)[None, :]).astype(
        jnp.bfloat16
    )
    piece = lax.all_gather(metric, "aux", axis=0, tiled=True)
    columns = piece.reshape(piece.shape[0], aux_count, block_size)
    ordered = jnp.einsum(
        "rgp,ag->rap", columns, aux_table, preferred_element_type=jnp.float32
    ).astype(jnp.bfloat16)
    fitted = jnp.einsum(
        "rap,iabpm->irbm", ordered, moved, preferred_element_type=jnp.float32
    ).astype(jnp.bfloat16)
    partial_value = jnp.einsum(
        "iqbm,iqcn->bmcn", fitted, fitted, preferred_element_type=jnp.float32
    )
    column_share = bas_count * block_size // (aux_count * occ_count)
    arranged = partial_value.reshape(bas_count, block_size, aux_count, occ_count, column_share)
    arranged = arranged.transpose(2, 0, 3, 1, 4).reshape(-1, column_share)
    return lax.psum_scatter(arranged, ("aux", "bas", "occ"), scatter_dimension=0, tiled=True)


def solution(mesh):
    in_specs = (
        P(("parts", "aux"), "bas", None, None, None, None),
        P(("parts", "aux"), "bas", None),
        P(("parts", "bas"), "occ"),
        P(("parts", "aux"), None),
        P("parts"),
    )
    out_specs = P(("parts", "bas"), ("aux", "occ"))
    small = mesh.shape["aux"] == 4 and mesh.shape["bas"] == 2 and mesh.shape["occ"] == 2
    return jax.shard_map(
        per_device if small else plain_device,
        mesh=mesh,
        in_specs=in_specs,
        out_specs=out_specs,
        check_vma=False,
    )
```

```python
import functools

import jax
import jax.numpy as jnp
from jax import lax
from jax.experimental import pallas as pl
from jax.experimental.pallas import tpu as pltpu
from jax.sharding import PartitionSpec as P

F32 = jnp.float32
BF16 = jnp.bfloat16
ROWS = 16
WINDOW = 5
GROUPS = ((0, 7), (7, 13), (13, 16))
FIRST = 32
OPEN = (4, 1, 5, 3, 6, 7)
ORDER = (
    ((2, -1), (4, 0), (5, 0), (1, 0), (6, 0), (2, 0), (7, 0), (3, 0))
    + ((4, 1), (5, 1), (7, 1), (6, 1))
    + ((7, 2), (4, 2), (5, 2), (6, 2))
)
RESTDEP = 1
LAST = (3, 2, 1)
WHOLE = pl.BlockSpec(memory_space=pltpu.VMEM)


def params(mib=40):
    return pltpu.CompilerParams(vmem_limit_bytes=mib * 2**20)


def cost(macs, size):
    return pl.CostEstimate(flops=2 * macs, bytes_accessed=size, transcendentals=0)


def relayout_kernel(x_ref, o_ref):
    slots, depth, rows, width = x_ref.shape
    o_ref[...] = jnp.swapaxes(x_ref[...].reshape(slots * depth, rows, width), 0, 1)


def relayout(integrals, first):
    slots, depth, _, width = integrals.shape
    return pl.pallas_call(
        relayout_kernel,
        grid=(first // ROWS,),
        in_specs=[pl.BlockSpec((slots, depth, ROWS, width), lambda j: (0, 0, j, 0))],
        out_specs=pl.BlockSpec((ROWS, slots * depth, width), lambda j: (j, 0, 0)),
        out_shape=jax.ShapeDtypeStruct((first, slots * depth, width), BF16),
        compiler_params=params(),
        cost_estimate=cost(0, 2 * first * slots * depth * width * 2),
        name="relayout",
    )(integrals)


def products(table, block):
    parts = []
    for p in range(0, block.shape[0], 2):
        pair = jnp.concatenate([block[p], block[p + 1]], axis=1)
        value = jnp.dot(table, pair, preferred_element_type=F32).astype(BF16)
        width = block.shape[2]
        parts += [value[:, :width], value[:, width:]]
    return jnp.swapaxes(jnp.stack(parts), 0, 1)


def first_kernel(chips, where, own_ref, other_ref, x_ref, *rest):
    outs, table_ref, plain = rest[:chips], rest[chips], rest[chips + 1]
    share = table_ref.shape[0] // chips
    block = plain.shape[0]
    held = own_ref.shape[0] // block
    for s in range(plain.shape[1] // block):
        name = where[0, 2 + s]
        away = lax.div(name, held) != where[0, 1]
        start = pl.multiple_of(lax.rem(name, held) * block, block)
        mine = own_ref[pl.ds(start, block), :].astype(F32)
        theirs = other_ref[pl.ds(start, block), :].astype(F32)
        picked = jnp.where(away, theirs, mine)
        plain[:, s * block : (s + 1) * block] = picked.T.astype(BF16)
    me = where[0, 0]
    for k in range(chips):
        start = pl.multiple_of((me ^ k) * share, share)
        table_ref[k * share : (k + 1) * share, :] = plain[pl.ds(start, share), :]
    for at in range(0, x_ref.shape[0], ROWS):
        value = products(table_ref[...], x_ref[at : at + ROWS])
        for k in range(chips):
            outs[k][:, at : at + ROWS, :] = value[k * share : (k + 1) * share]


def first_products(chips, where, own, other, moved, first):
    _, depth, width = moved.shape
    orbitals = own.shape[1]
    share = orbitals // chips
    return pl.pallas_call(
        functools.partial(first_kernel, chips),
        in_specs=[WHOLE] * 4,
        out_specs=[WHOLE] * (chips + 1),
        out_shape=[jax.ShapeDtypeStruct((share, first, width), BF16)] * chips
        + [jax.ShapeDtypeStruct((orbitals, depth), BF16)],
        scratch_shapes=[pltpu.VMEM((orbitals, depth), BF16)],
        compiler_params=params(),
        cost_estimate=cost(orbitals * depth * first * width, moved.size * 2),
        name="first_products",
    )(where[None], own, other, moved)


def rest_kernel(chips, spans, x_ref, table_ref, _, *outs):
    slots, depth, rows, width = x_ref.shape
    block = jnp.swapaxes(x_ref[...].reshape(slots * depth, rows, width), 0, 1)
    value = products(table_ref[...], block)
    share = table_ref.shape[0] // chips
    for (k, lo, hi), out in zip(spans, outs):
        out[...] = value[k * share + lo : k * share + hi]


def rest_products(chips, spans, integrals, table, first, after):
    slots, depth, total, width = integrals.shape
    orbitals = table.shape[0]
    rest = total - first
    skip = first // ROWS
    shapes = [hi - lo for _, lo, hi in spans]
    return pl.pallas_call(
        functools.partial(rest_kernel, chips, spans),
        grid=(rest // ROWS,),
        in_specs=[
            pl.BlockSpec((slots, depth, ROWS, width), lambda j: (0, 0, j + skip, 0)),
            pl.BlockSpec(table.shape, lambda j: (0, 0)),
            pl.BlockSpec(memory_space=pl.ANY),
        ],
        out_specs=[pl.BlockSpec((n, ROWS, width), lambda j: (0, j, 0)) for n in shapes],
        out_shape=[jax.ShapeDtypeStruct((n, rest, width), BF16) for n in shapes],
        compiler_params=params(),
        cost_estimate=cost(orbitals * table.shape[1] * rest * width, integrals.size * 2),
        name="rest_products",
    )(integrals, table, after)


def metric_kernel(where, *refs):
    o_ref = refs[-1]
    aux = where.shape[0] - 1
    width = o_ref.shape[1] // aux
    for kz in range(aux):
        start = pl.multiple_of(where[where[aux] ^ kz] * width, width)
        at = 0
        for ref in refs[:-1]:
            size = ref.shape[0]
            o_ref[at : at + size, kz * width : (kz + 1) * width] = ref[:, pl.ds(start, width)]
            at += size


def ordered_metric(where, pieces):
    total = sum(piece.shape[0] for piece in pieces)
    columns = pieces[0].shape[1]
    return pl.pallas_call(
        metric_kernel,
        in_specs=[pl.BlockSpec(memory_space=pltpu.SMEM)] + [WHOLE] * len(pieces),
        out_specs=WHOLE,
        out_shape=jax.ShapeDtypeStruct((total, columns), BF16),
        compiler_params=params(),
        cost_estimate=cost(0, total * columns * 4),
        name="ordered_metric",
    )(where, *pieces)


def add_group(aux, bas, lo, hi, starts, metric, early, late, total):
    chips = aux * bas
    fitted = []
    for i in range(lo, hi):
        columns = []
        for k in range(chips):
            columns.append(jnp.concatenate([early[k][i], late[k][starts[k] + i - lo]], axis=0))
        stacked = jnp.concatenate(
            [jnp.concatenate(columns[kz * bas : (kz + 1) * bas], axis=1) for kz in range(aux)],
            axis=0,
        )
        fitted.append(jnp.dot(metric, stacked, preferred_element_type=F32).astype(BF16))
    fitted = jnp.concatenate(fitted, axis=0)
    return total + lax.dot_general(
        fitted, fitted, (((0,), (0,)), ((), ())), preferred_element_type=F32
    )


def group_kernel(aux, bas, lo, hi, starts, started, last, *refs):
    chips = aux * bas
    refs = list(refs)
    where = refs.pop(0) if last else None
    metric = refs.pop(0)[...]
    early = [refs.pop(0) for _ in range(chips)]
    late = [refs.pop(0) for _ in range(chips)]
    side = bas * late[0].shape[2]
    total = refs.pop(0)[...] if started else jnp.zeros((side, side), F32)
    total = add_group(aux, bas, lo, hi, starts, metric, early, late, total)
    if not last:
        refs[0][...] = total
        return
    kept, near, away, scratch = refs
    scratch[...] = total
    width = side // bas
    piece = kept.shape[1]
    a_here, b_here, o_here = (where[0, n] for n in range(3))
    for ka in range(aux):
        a = a_here ^ ka
        for who in range(2):
            row = (a * 2 + (o_here ^ who)) * piece
            block = lax.div(row, width) ^ b_here
            start = pl.multiple_of(block * width + lax.rem(row, width), piece)
            value = scratch[pl.ds(start, piece), :]
            if who:
                away[ka] = value
            else:
                kept[ka] = value[:, :width]
                near[ka] = value[:, width:]


def group(aux, bas, lo, hi, metric, early, late, total, where=None):
    starts = tuple(start for _, start in late)
    late = [value for value, _ in late]
    last, started = where is not None, total is not None
    width = late[0].shape[2]
    side = bas * width
    args = ([where[None]] if last else []) + [metric, *early, *late] + ([total] if started else [])
    specs = [WHOLE] * len(args)
    if last:
        piece = side // (aux * 2)
        out = [
            jax.ShapeDtypeStruct((aux, piece, width), F32),
            jax.ShapeDtypeStruct((aux, piece, width), F32),
            jax.ShapeDtypeStruct((aux, piece, side), F32),
        ]
    else:
        out = jax.ShapeDtypeStruct((side, side), F32)
    rows = metric.shape[0]
    macs = (hi - lo) * (rows * rows * side + rows * side * side)
    return pl.pallas_call(
        functools.partial(group_kernel, aux, bas, lo, hi, starts, started, last),
        in_specs=specs,
        out_specs=[WHOLE] * 3 if last else WHOLE,
        out_shape=out,
        scratch_shapes=[pltpu.VMEM((side, side), F32)] if last else [],
        compiler_params=params(),
        cost_estimate=cost(macs, (hi - lo) * rows * side * 2),
        name="group",
    )(*args)


def per_device(integrals, screening, coefficients, metric, aux_owner):
    aux = lax.axis_size("aux")
    bas = lax.axis_size("bas")
    chips = aux * bas
    integrals = integrals[0, 0]
    orbitals = coefficients.shape[1]
    share = orbitals // chips
    a, b, o = (lax.axis_index(name) for name in ("aux", "bas", "occ"))
    first = FIRST
    groups = GROUPS
    inner, outer = (1, 2, 3), (4, 5, 6, 7)

    def swap(value, kz=0, kx=0):
        pairs = [
            (i * bas + j, (i ^ kz) * bas + (j ^ kx)) for i in range(aux) for j in range(bas)
        ]
        return lax.ppermute(value, ("aux", "bas"), pairs)

    def across(value):
        return lax.ppermute(value, "occ", [(0, 1), (1, 0)])

    def after(value, *earlier):
        return lax.optimization_barrier((value, *earlier))[0]

    integrals = pltpu.with_memory_space_constraint(integrals, pltpu.HBM)
    other = swap(coefficients, kx=1)
    moved = relayout(integrals, first)
    where = jnp.concatenate([jnp.stack([a * bas + b, b]), screening[0, 0]]).astype(jnp.int32)
    rows = metric.shape[0] // 4
    held = lax.dynamic_slice_in_dim(metric, (b * 2 + o) * rows, rows, axis=0)
    held = [held, swap(held, kz=2)]
    *early, table = first_products(
        chips, where, after(coefficients, *held), other, moved, first
    )
    held = jnp.concatenate(held, axis=0)
    sent = []

    def send(value, kz, kx):
        if len(sent) >= WINDOW:
            value = after(value, sent[-WINDOW])
        sent.append(swap(value, kz, kx))
        return sent[-1]

    got = {(k, -1): send(early[k], k // bas, k % bas) for k in OPEN}
    got[0, -1] = early[0]
    spans = [(k, lo, hi) for lo, hi in groups for k in outer]
    spans += [(k, 0, share) for k in (0, *inner)]
    late = rest_products(chips, tuple(spans), integrals, table, first, got[RESTDEP, -1])
    made = dict(zip(spans, late))
    got[0, 0] = made[0, 0, share]
    for k, g in ORDER:
        if g < 0:
            value = after(early[k], late[0])
        else:
            value = made[(k, *groups[g])] if k in outer else made[k, 0, share]
        got[k, g] = send(value, k // bas, k % bas)
    held = jnp.concatenate([held, swap(held, kz=1)], axis=0)
    held = jnp.concatenate([held, swap(held, kx=1)], axis=0)
    ordered = ordered_metric(
        jnp.concatenate([aux_owner, a[None]]).astype(jnp.int32), [held, across(held)]
    )
    early = [got[k, -1] for k in range(chips)]
    total = None
    for g, (lo, hi) in enumerate(groups):
        part = [
            (got[k, g], 0) if k in outer else (got[k, 0], lo) for k in range(chips)
        ]
        place = jnp.stack([a, b, o]).astype(jnp.int32) if g == len(groups) - 1 else None
        total = group(aux, bas, lo, hi, ordered, early, part, total, place)
    kept, near, away = total
    away = across(away)
    width = kept.shape[2]
    kept = kept + away[:, :, :width]
    near = near + away[:, :, width:]
    kept = kept + swap(near, kx=1)
    value = kept[0]
    for kz in LAST:
        value = value + swap(kept[kz], kz=kz)
    return value.T


def plain_device(integrals, screening, coefficients, metric, aux_owner):
    block_size = integrals.shape[-1]
    aux_count = lax.axis_size("aux")
    bas_count = lax.axis_size("bas")
    occ_count = lax.axis_size("occ")
    gathered = lax.all_gather(coefficients, "bas", axis=0, tiled=True)
    orbitals = gathered.shape[1]
    by_block = gathered.reshape(gathered.shape[0] // block_size, block_size, orbitals)
    picked = jnp.take(by_block, screening[0, 0], axis=0)
    stacked = integrals[0, 0].reshape(integrals.shape[2], block_size, block_size * block_size)
    contracted = lax.dot_general(
        picked, stacked, (((0, 1), (0, 1)), ((), ())), preferred_element_type=jnp.float32
    )
    transformed = contracted.astype(jnp.bfloat16)
    share = orbitals // (aux_count * bas_count)
    moved = lax.all_to_all(
        transformed.reshape(orbitals, 1, block_size, block_size),
        ("aux", "bas"),
        split_axis=0,
        concat_axis=1,
        tiled=True,
    )
    moved = moved.reshape(share, aux_count, bas_count, block_size, block_size)
    aux_table = (aux_owner[:, None] == jnp.arange(aux_count, dtype=jnp.int32)[None, :]).astype(
        jnp.bfloat16
    )
    piece = lax.all_gather(metric, "aux", axis=0, tiled=True)
    columns = piece.reshape(piece.shape[0], aux_count, block_size)
    ordered = jnp.einsum(
        "rgp,ag->rap", columns, aux_table, preferred_element_type=jnp.float32
    ).astype(jnp.bfloat16)
    fitted = jnp.einsum(
        "rap,iabpm->irbm", ordered, moved, preferred_element_type=jnp.float32
    ).astype(jnp.bfloat16)
    partial_value = jnp.einsum(
        "iqbm,iqcn->bmcn", fitted, fitted, preferred_element_type=jnp.float32
    )
    column_share = bas_count * block_size // (aux_count * occ_count)
    arranged = partial_value.reshape(bas_count, block_size, aux_count, occ_count, column_share)
    arranged = arranged.transpose(2, 0, 3, 1, 4).reshape(-1, column_share)
    return lax.psum_scatter(arranged, ("aux", "bas", "occ"), scatter_dimension=0, tiled=True)


def solution(mesh):
    in_specs = (
        P(("parts", "aux"), "bas", None, None, None, None),
        P(("parts", "aux"), "bas", None),
        P(("parts", "bas"), "occ"),
        P(("parts", "aux"), None),
        P("parts"),
    )
    out_specs = P(("parts", "bas"), ("aux", "occ"))
    small = mesh.shape["aux"] == 4 and mesh.shape["bas"] == 2 and mesh.shape["occ"] == 2
    return jax.shard_map(
        per_device if small else plain_device,
        mesh=mesh,
        in_specs=in_specs,
        out_specs=out_specs,
        check_vma=False,
    )
```

```python
import functools

import jax
import jax.numpy as jnp
from jax import lax
from jax.experimental import pallas as pl
from jax.experimental.pallas import tpu as pltpu
from jax.sharding import PartitionSpec as P

F32 = jnp.float32
BF16 = jnp.bfloat16
ROWS = 16
WINDOW = 5
GROUPS = ((0, 7), (7, 13), (13, 16))
FIRST = 32
OPEN = (6, 1, 5, 3, 4, 7)
ORDER = (
    ((2, -1), (5, 0), (4, 0), (1, 0), (6, 0), (2, 0), (7, 0), (3, 0))
    + ((4, 1), (5, 1), (7, 1), (6, 1))
    + ((7, 2), (4, 2), (5, 2), (6, 2))
)
RESTDEP = 1
LAST = (3, 1, 2)
WHOLE = pl.BlockSpec(memory_space=pltpu.VMEM)


def params(mib=40):
    return pltpu.CompilerParams(vmem_limit_bytes=mib * 2**20)


def cost(macs, size):
    return pl.CostEstimate(flops=2 * macs, bytes_accessed=size, transcendentals=0)


def relayout_kernel(x_ref, o_ref):
    slots, depth, rows, width = x_ref.shape
    o_ref[...] = jnp.swapaxes(x_ref[...].reshape(slots * depth, rows, width), 0, 1)


def relayout(integrals, first):
    slots, depth, _, width = integrals.shape
    return pl.pallas_call(
        relayout_kernel,
        grid=(first // ROWS,),
        in_specs=[pl.BlockSpec((slots, depth, ROWS, width), lambda j: (0, 0, j, 0))],
        out_specs=pl.BlockSpec((ROWS, slots * depth, width), lambda j: (j, 0, 0)),
        out_shape=jax.ShapeDtypeStruct((first, slots * depth, width), BF16),
        compiler_params=params(),
        cost_estimate=cost(0, 2 * first * slots * depth * width * 2),
        name="relayout",
    )(integrals)


def products(table, block):
    parts = []
    for p in range(0, block.shape[0], 2):
        pair = jnp.concatenate([block[p], block[p + 1]], axis=1)
        value = jnp.dot(table, pair, preferred_element_type=F32).astype(BF16)
        width = block.shape[2]
        parts += [value[:, :width], value[:, width:]]
    return jnp.swapaxes(jnp.stack(parts), 0, 1)


def first_kernel(chips, where, own_ref, other_ref, x_ref, *rest):
    outs, table_ref, plain = rest[:chips], rest[chips], rest[chips + 1]
    share = table_ref.shape[0] // chips
    block = plain.shape[0]
    held = own_ref.shape[0] // block
    for s in range(plain.shape[1] // block):
        name = where[0, 2 + s]
        away = lax.div(name, held) != where[0, 1]
        start = pl.multiple_of(lax.rem(name, held) * block, block)
        mine = own_ref[pl.ds(start, block), :].astype(F32)
        theirs = other_ref[pl.ds(start, block), :].astype(F32)
        picked = jnp.where(away, theirs, mine)
        plain[:, s * block : (s + 1) * block] = picked.T.astype(BF16)
    me = where[0, 0]
    for k in range(chips):
        start = pl.multiple_of((me ^ k) * share, share)
        table_ref[k * share : (k + 1) * share, :] = plain[pl.ds(start, share), :]
    for at in range(0, x_ref.shape[0], ROWS):
        value = products(table_ref[...], x_ref[at : at + ROWS])
        for k in range(chips):
            outs[k][:, at : at + ROWS, :] = value[k * share : (k + 1) * share]


def first_products(chips, where, own, other, moved, first):
    _, depth, width = moved.shape
    orbitals = own.shape[1]
    share = orbitals // chips
    return pl.pallas_call(
        functools.partial(first_kernel, chips),
        in_specs=[WHOLE] * 4,
        out_specs=[WHOLE] * (chips + 1),
        out_shape=[jax.ShapeDtypeStruct((share, first, width), BF16)] * chips
        + [jax.ShapeDtypeStruct((orbitals, depth), BF16)],
        scratch_shapes=[pltpu.VMEM((orbitals, depth), BF16)],
        compiler_params=params(),
        cost_estimate=cost(orbitals * depth * first * width, moved.size * 2),
        name="first_products",
    )(where[None], own, other, moved)


def rest_kernel(chips, spans, x_ref, table_ref, _, *outs):
    slots, depth, rows, width = x_ref.shape
    block = jnp.swapaxes(x_ref[...].reshape(slots * depth, rows, width), 0, 1)
    value = products(table_ref[...], block)
    share = table_ref.shape[0] // chips
    for (k, lo, hi), out in zip(spans, outs):
        out[...] = value[k * share + lo : k * share + hi]


def rest_products(chips, spans, integrals, table, first, after):
    slots, depth, total, width = integrals.shape
    orbitals = table.shape[0]
    rest = total - first
    skip = first // ROWS
    shapes = [hi - lo for _, lo, hi in spans]
    return pl.pallas_call(
        functools.partial(rest_kernel, chips, spans),
        grid=(rest // ROWS,),
        in_specs=[
            pl.BlockSpec((slots, depth, ROWS, width), lambda j: (0, 0, j + skip, 0)),
            pl.BlockSpec(table.shape, lambda j: (0, 0)),
            pl.BlockSpec(memory_space=pl.ANY),
        ],
        out_specs=[pl.BlockSpec((n, ROWS, width), lambda j: (0, j, 0)) for n in shapes],
        out_shape=[jax.ShapeDtypeStruct((n, rest, width), BF16) for n in shapes],
        compiler_params=params(),
        cost_estimate=cost(orbitals * table.shape[1] * rest * width, integrals.size * 2),
        name="rest_products",
    )(integrals, table, after)


def metric_kernel(where, *refs):
    o_ref = refs[-1]
    aux = where.shape[0] - 1
    width = o_ref.shape[1] // aux
    for kz in range(aux):
        start = pl.multiple_of(where[where[aux] ^ kz] * width, width)
        at = 0
        for ref in refs[:-1]:
            size = ref.shape[0]
            o_ref[at : at + size, kz * width : (kz + 1) * width] = ref[:, pl.ds(start, width)]
            at += size


def ordered_metric(where, pieces):
    total = sum(piece.shape[0] for piece in pieces)
    columns = pieces[0].shape[1]
    return pl.pallas_call(
        metric_kernel,
        in_specs=[pl.BlockSpec(memory_space=pltpu.SMEM)] + [WHOLE] * len(pieces),
        out_specs=WHOLE,
        out_shape=jax.ShapeDtypeStruct((total, columns), BF16),
        compiler_params=params(),
        cost_estimate=cost(0, total * columns * 4),
        name="ordered_metric",
    )(where, *pieces)


def add_group(aux, bas, lo, hi, starts, metric, early, late, total):
    chips = aux * bas
    fitted = []
    for i in range(lo, hi):
        columns = []
        for k in range(chips):
            columns.append(jnp.concatenate([early[k][i], late[k][starts[k] + i - lo]], axis=0))
        stacked = jnp.concatenate(
            [jnp.concatenate(columns[kz * bas : (kz + 1) * bas], axis=1) for kz in range(aux)],
            axis=0,
        )
        fitted.append(jnp.dot(metric, stacked, preferred_element_type=F32).astype(BF16))
    fitted = jnp.concatenate(fitted, axis=0)
    return total + lax.dot_general(
        fitted, fitted, (((0,), (0,)), ((), ())), preferred_element_type=F32
    )


def group_kernel(aux, bas, lo, hi, starts, started, last, *refs):
    chips = aux * bas
    refs = list(refs)
    where = refs.pop(0) if last else None
    metric = refs.pop(0)[...]
    early = [refs.pop(0) for _ in range(chips)]
    late = [refs.pop(0) for _ in range(chips)]
    side = bas * late[0].shape[2]
    total = refs.pop(0)[...] if started else jnp.zeros((side, side), F32)
    total = add_group(aux, bas, lo, hi, starts, metric, early, late, total)
    if not last:
        refs[0][...] = total
        return
    kept, near, kept_away, near_away, scratch = refs
    scratch[...] = total
    width = side // bas
    piece = kept.shape[1]
    a_here, b_here, o_here = (where[0, n] for n in range(3))
    for ka in range(aux):
        a = a_here ^ ka
        for who in range(2):
            row = (a * 2 + (o_here ^ who)) * piece
            block = lax.div(row, width) ^ b_here
            start = pl.multiple_of(block * width + lax.rem(row, width), piece)
            value = scratch[pl.ds(start, piece), :]
            (kept_away if who else kept)[ka] = value[:, :width]
            (near_away if who else near)[ka] = value[:, width:]


def group(aux, bas, lo, hi, metric, early, late, total, where=None):
    starts = tuple(start for _, start in late)
    late = [value for value, _ in late]
    last, started = where is not None, total is not None
    width = late[0].shape[2]
    side = bas * width
    args = ([where[None]] if last else []) + [metric, *early, *late] + ([total] if started else [])
    specs = [WHOLE] * len(args)
    if last:
        piece = side // (aux * 2)
        out = [jax.ShapeDtypeStruct((aux, piece, width), F32)] * 4
    else:
        out = jax.ShapeDtypeStruct((side, side), F32)
    rows = metric.shape[0]
    macs = (hi - lo) * (rows * rows * side + rows * side * side)
    return pl.pallas_call(
        functools.partial(group_kernel, aux, bas, lo, hi, starts, started, last),
        in_specs=specs,
        out_specs=[WHOLE] * 4 if last else WHOLE,
        out_shape=out,
        scratch_shapes=[pltpu.VMEM((side, side), F32)] if last else [],
        compiler_params=params(),
        cost_estimate=cost(macs, (hi - lo) * rows * side * 2),
        name="group",
    )(*args)


def per_device(integrals, screening, coefficients, metric, aux_owner):
    aux = lax.axis_size("aux")
    bas = lax.axis_size("bas")
    chips = aux * bas
    integrals = integrals[0, 0]
    orbitals = coefficients.shape[1]
    share = orbitals // chips
    a, b, o = (lax.axis_index(name) for name in ("aux", "bas", "occ"))
    first, groups = FIRST, GROUPS
    inner, outer = (1, 2, 3), (4, 5, 6, 7)

    def swap(value, kz=0, kx=0):
        pairs = [
            (i * bas + j, (i ^ kz) * bas + (j ^ kx)) for i in range(aux) for j in range(bas)
        ]
        return lax.ppermute(value, ("aux", "bas"), pairs)

    def across(value):
        return lax.ppermute(value, "occ", [(0, 1), (1, 0)])

    def after(value, *earlier):
        return lax.optimization_barrier((value, *earlier))[0]

    integrals = pltpu.with_memory_space_constraint(integrals, pltpu.HBM)
    other = swap(coefficients, kx=1)
    moved = relayout(integrals, first)
    where = jnp.concatenate([jnp.stack([a * bas + b, b]), screening[0, 0]]).astype(jnp.int32)
    rows = metric.shape[0] // 4
    held = lax.dynamic_slice_in_dim(metric, (b * 2 + o) * rows, rows, axis=0)
    held = [held, swap(held, kz=2)]
    *early, table = first_products(
        chips, where, after(coefficients, *held), other, moved, first
    )
    held = jnp.concatenate(held, axis=0)
    sent = []

    def send(value, kz, kx):
        if len(sent) >= WINDOW:
            value = after(value, sent[-WINDOW])
        sent.append(swap(value, kz, kx))
        return sent[-1]

    got = {(k, -1): send(early[k], k // bas, k % bas) for k in OPEN}
    got[0, -1] = early[0]
    spans = [(k, lo, hi) for lo, hi in groups for k in outer]
    spans += [(k, 0, share) for k in (0, *inner)]
    late = rest_products(chips, tuple(spans), integrals, table, first, got[RESTDEP, -1])
    made = dict(zip(spans, late))
    got[0, 0] = made[0, 0, share]
    for k, g in ORDER:
        if g < 0:
            value = after(early[k], late[0])
        else:
            value = made[(k, *groups[g])] if k in outer else made[k, 0, share]
        got[k, g] = send(value, k // bas, k % bas)
    held = jnp.concatenate([held, swap(held, kz=1)], axis=0)
    held = jnp.concatenate([held, swap(held, kx=1)], axis=0)
    ordered = ordered_metric(
        jnp.concatenate([aux_owner, a[None]]).astype(jnp.int32), [held, across(held)]
    )
    early = [got[k, -1] for k in range(chips)]
    total = None
    for g, (lo, hi) in enumerate(groups):
        part = [
            (got[k, g], 0) if k in outer else (got[k, 0], lo) for k in range(chips)
        ]
        place = jnp.stack([a, b, o]).astype(jnp.int32) if g == len(groups) - 1 else None
        total = group(aux, bas, lo, hi, ordered, early, part, total, place)
    kept, near, kept_away, near_away = total
    near = near + across(near_away)
    near = swap(near, kx=1)
    kept = kept + across(kept_away)
    kept = kept + near
    value = kept[0]
    for kz in LAST:
        value = value + swap(kept[kz], kz=kz)
    return value.T


def plain_device(integrals, screening, coefficients, metric, aux_owner):
    block_size = integrals.shape[-1]
    aux_count = lax.axis_size("aux")
    bas_count = lax.axis_size("bas")
    occ_count = lax.axis_size("occ")
    gathered = lax.all_gather(coefficients, "bas", axis=0, tiled=True)
    orbitals = gathered.shape[1]
    by_block = gathered.reshape(gathered.shape[0] // block_size, block_size, orbitals)
    picked = jnp.take(by_block, screening[0, 0], axis=0)
    stacked = integrals[0, 0].reshape(integrals.shape[2], block_size, block_size * block_size)
    contracted = lax.dot_general(
        picked, stacked, (((0, 1), (0, 1)), ((), ())), preferred_element_type=jnp.float32
    )
    transformed = contracted.astype(jnp.bfloat16)
    share = orbitals // (aux_count * bas_count)
    moved = lax.all_to_all(
        transformed.reshape(orbitals, 1, block_size, block_size),
        ("aux", "bas"),
        split_axis=0,
        concat_axis=1,
        tiled=True,
    )
    moved = moved.reshape(share, aux_count, bas_count, block_size, block_size)
    aux_table = (aux_owner[:, None] == jnp.arange(aux_count, dtype=jnp.int32)[None, :]).astype(
        jnp.bfloat16
    )
    piece = lax.all_gather(metric, "aux", axis=0, tiled=True)
    columns = piece.reshape(piece.shape[0], aux_count, block_size)
    ordered = jnp.einsum(
        "rgp,ag->rap", columns, aux_table, preferred_element_type=jnp.float32
    ).astype(jnp.bfloat16)
    fitted = jnp.einsum(
        "rap,iabpm->irbm", ordered, moved, preferred_element_type=jnp.float32
    ).astype(jnp.bfloat16)
    partial_value = jnp.einsum(
        "iqbm,iqcn->bmcn", fitted, fitted, preferred_element_type=jnp.float32
    )
    column_share = bas_count * block_size // (aux_count * occ_count)
    arranged = partial_value.reshape(bas_count, block_size, aux_count, occ_count, column_share)
    arranged = arranged.transpose(2, 0, 3, 1, 4).reshape(-1, column_share)
    return lax.psum_scatter(arranged, ("aux", "bas", "occ"), scatter_dimension=0, tiled=True)


def solution(mesh):
    in_specs = (
        P(("parts", "aux"), "bas", None, None, None, None),
        P(("parts", "aux"), "bas", None),
        P(("parts", "bas"), "occ"),
        P(("parts", "aux"), None),
        P("parts"),
    )
    out_specs = P(("parts", "bas"), ("aux", "occ"))
    small = mesh.shape["aux"] == 4 and mesh.shape["bas"] == 2 and mesh.shape["occ"] == 2
    return jax.shard_map(
        per_device if small else plain_device,
        mesh=mesh,
        in_specs=in_specs,
        out_specs=out_specs,
        check_vma=False,
    )
```

```python
import functools

import jax
import jax.numpy as jnp
from jax import lax
from jax.experimental import pallas as pl
from jax.experimental.pallas import tpu as pltpu
from jax.sharding import PartitionSpec as P

F32 = jnp.float32
BF16 = jnp.bfloat16
ROWS = 16
WINDOW = 5
GROUPS = ((0, 7), (7, 13), (13, 16))
FIRST = 32
OPEN = (6, 1, 5, 3, 4, 7)
ORDER = (
    ((2, -1), (5, 0), (4, 0), (1, 0), (6, 0), (2, 0), (7, 0), (3, 0))
    + ((4, 1), (5, 1), (7, 1), (6, 1))
    + ((7, 2), (4, 2), (5, 2), (6, 2))
)
RESTDEP = 1
LAST = (3, 1, 2)
WHOLE = pl.BlockSpec(memory_space=pltpu.VMEM)


def params(mib=40):
    return pltpu.CompilerParams(vmem_limit_bytes=mib * 2**20)


def cost(macs, size):
    return pl.CostEstimate(flops=2 * macs, bytes_accessed=size, transcendentals=0)


def relayout_kernel(x_ref, o_ref):
    slots, depth, rows, width = x_ref.shape
    o_ref[...] = jnp.swapaxes(x_ref[...].reshape(slots * depth, rows, width), 0, 1)


def relayout(integrals, first):
    slots, depth, _, width = integrals.shape
    return pl.pallas_call(
        relayout_kernel,
        grid=(first // ROWS,),
        in_specs=[pl.BlockSpec((slots, depth, ROWS, width), lambda j: (0, 0, j, 0))],
        out_specs=pl.BlockSpec((ROWS, slots * depth, width), lambda j: (j, 0, 0)),
        out_shape=jax.ShapeDtypeStruct((first, slots * depth, width), BF16),
        compiler_params=params(),
        cost_estimate=cost(0, 2 * first * slots * depth * width * 2),
        name="relayout",
    )(integrals)


def products(table, block):
    parts = []
    for p in range(0, block.shape[0], 2):
        pair = jnp.concatenate([block[p], block[p + 1]], axis=1)
        value = jnp.dot(table, pair, preferred_element_type=F32).astype(BF16)
        width = block.shape[2]
        parts += [value[:, :width], value[:, width:]]
    return jnp.swapaxes(jnp.stack(parts), 0, 1)


def first_kernel(chips, where, own_ref, other_ref, x_ref, *rest):
    outs, table_ref, plain = rest[:chips], rest[chips], rest[chips + 1]
    share = table_ref.shape[0] // chips
    block = plain.shape[0]
    held = own_ref.shape[0] // block
    for s in range(plain.shape[1] // block):
        name = where[0, 2 + s]
        away = lax.div(name, held) != where[0, 1]
        start = pl.multiple_of(lax.rem(name, held) * block, block)
        mine = own_ref[pl.ds(start, block), :]
        theirs = other_ref[pl.ds(start, block), :]
        picked = jnp.where(away, theirs, mine)
        plain[:, s * block : (s + 1) * block] = picked.T
    me = where[0, 0]
    for k in range(chips):
        start = pl.multiple_of((me ^ k) * share, share)
        table_ref[k * share : (k + 1) * share, :] = plain[pl.ds(start, share), :]
    for at in range(0, x_ref.shape[0], ROWS):
        value = products(table_ref[...], x_ref[at : at + ROWS])
        for k in range(chips):
            outs[k][:, at : at + ROWS, :] = value[k * share : (k + 1) * share]


def first_products(chips, where, own, other, moved, first):
    _, depth, width = moved.shape
    orbitals = own.shape[1]
    share = orbitals // chips
    return pl.pallas_call(
        functools.partial(first_kernel, chips),
        in_specs=[WHOLE] * 4,
        out_specs=[WHOLE] * (chips + 1),
        out_shape=[jax.ShapeDtypeStruct((share, first, width), BF16)] * chips
        + [jax.ShapeDtypeStruct((orbitals, depth), BF16)],
        scratch_shapes=[pltpu.VMEM((orbitals, depth), BF16)],
        compiler_params=params(),
        cost_estimate=cost(orbitals * depth * first * width, moved.size * 2),
        name="first_products",
    )(where[None], own, other, moved)


def rest_kernel(chips, spans, x_ref, table_ref, _, *outs):
    slots, depth, rows, width = x_ref.shape
    block = jnp.swapaxes(x_ref[...].reshape(slots * depth, rows, width), 0, 1)
    value = products(table_ref[...], block)
    share = table_ref.shape[0] // chips
    for (k, lo, hi), out in zip(spans, outs):
        out[...] = value[k * share + lo : k * share + hi]


def rest_products(chips, spans, integrals, table, first, after):
    slots, depth, total, width = integrals.shape
    orbitals = table.shape[0]
    rest = total - first
    skip = first // ROWS
    shapes = [hi - lo for _, lo, hi in spans]
    return pl.pallas_call(
        functools.partial(rest_kernel, chips, spans),
        grid=(rest // ROWS,),
        in_specs=[
            pl.BlockSpec((slots, depth, ROWS, width), lambda j: (0, 0, j + skip, 0)),
            pl.BlockSpec(table.shape, lambda j: (0, 0)),
            pl.BlockSpec(memory_space=pl.ANY),
        ],
        out_specs=[pl.BlockSpec((n, ROWS, width), lambda j: (0, j, 0)) for n in shapes],
        out_shape=[jax.ShapeDtypeStruct((n, rest, width), BF16) for n in shapes],
        compiler_params=params(),
        cost_estimate=cost(orbitals * table.shape[1] * rest * width, integrals.size * 2),
        name="rest_products",
    )(integrals, table, after)


def metric_kernel(where, *refs):
    o_ref = refs[-1]
    aux = where.shape[0] - 1
    width = o_ref.shape[1] // aux
    for kz in range(aux):
        start = pl.multiple_of(where[where[aux] ^ kz] * width, width)
        at = 0
        for ref in refs[:-1]:
            size = ref.shape[0]
            o_ref[at : at + size, kz * width : (kz + 1) * width] = ref[:, pl.ds(start, width)]
            at += size


def ordered_metric(where, pieces):
    total = sum(piece.shape[0] for piece in pieces)
    columns = pieces[0].shape[1]
    return pl.pallas_call(
        metric_kernel,
        in_specs=[pl.BlockSpec(memory_space=pltpu.SMEM)] + [WHOLE] * len(pieces),
        out_specs=WHOLE,
        out_shape=jax.ShapeDtypeStruct((total, columns), BF16),
        compiler_params=params(),
        cost_estimate=cost(0, total * columns * 4),
        name="ordered_metric",
    )(where, *pieces)


def add_group(aux, bas, lo, hi, starts, metric, early, late, total):
    chips = aux * bas
    fitted = []
    for i in range(lo, hi):
        columns = []
        for k in range(chips):
            columns.append(jnp.concatenate([early[k][i], late[k][starts[k] + i - lo]], axis=0))
        stacked = jnp.concatenate(
            [jnp.concatenate(columns[kz * bas : (kz + 1) * bas], axis=1) for kz in range(aux)],
            axis=0,
        )
        fitted.append(jnp.dot(metric, stacked, preferred_element_type=F32).astype(BF16))
    fitted = jnp.concatenate(fitted, axis=0)
    return total + lax.dot_general(
        fitted, fitted, (((0,), (0,)), ((), ())), preferred_element_type=F32
    )


def group_kernel(aux, bas, lo, hi, starts, started, last, *refs):
    chips = aux * bas
    refs = list(refs)
    where = refs.pop(0) if last else None
    metric = refs.pop(0)[...]
    early = [refs.pop(0) for _ in range(chips)]
    late = [refs.pop(0) for _ in range(chips)]
    side = bas * late[0].shape[2]
    total = refs.pop(0)[...] if started else jnp.zeros((side, side), F32)
    total = add_group(aux, bas, lo, hi, starts, metric, early, late, total)
    if not last:
        refs[0][...] = total
        return
    kept, near, kept_away, near_away, scratch = refs
    scratch[...] = total
    width = side // bas
    piece = kept.shape[1]
    a_here, b_here, o_here = (where[0, n] for n in range(3))
    for ka in range(aux):
        a = a_here ^ ka
        for who in range(2):
            row = (a * 2 + (o_here ^ who)) * piece
            block = lax.div(row, width) ^ b_here
            start = pl.multiple_of(block * width + lax.rem(row, width), piece)
            value = scratch[pl.ds(start, piece), :]
            (kept_away if who else kept)[ka] = value[:, :width]
            (near_away if who else near)[ka] = value[:, width:]


def group(aux, bas, lo, hi, metric, early, late, total, where=None):
    starts = tuple(start for _, start in late)
    late = [value for value, _ in late]
    last, started = where is not None, total is not None
    width = late[0].shape[2]
    side = bas * width
    args = ([where[None]] if last else []) + [metric, *early, *late] + ([total] if started else [])
    specs = [WHOLE] * len(args)
    if last:
        piece = side // (aux * 2)
        out = [jax.ShapeDtypeStruct((aux, piece, width), F32)] * 4
    else:
        out = jax.ShapeDtypeStruct((side, side), F32)
    rows = metric.shape[0]
    macs = (hi - lo) * (rows * rows * side + rows * side * side)
    return pl.pallas_call(
        functools.partial(group_kernel, aux, bas, lo, hi, starts, started, last),
        in_specs=specs,
        out_specs=[WHOLE] * 4 if last else WHOLE,
        out_shape=out,
        scratch_shapes=[pltpu.VMEM((side, side), F32)] if last else [],
        compiler_params=params(),
        cost_estimate=cost(macs, (hi - lo) * rows * side * 2),
        name="group",
    )(*args)


def per_device(integrals, screening, coefficients, metric, aux_owner):
    aux = lax.axis_size("aux")
    bas = lax.axis_size("bas")
    chips = aux * bas
    integrals = integrals[0, 0]
    orbitals = coefficients.shape[1]
    share = orbitals // chips
    a, b, o = (lax.axis_index(name) for name in ("aux", "bas", "occ"))
    first, groups = FIRST, GROUPS
    inner, outer = (1, 2, 3), (4, 5, 6, 7)

    def swap(value, kz=0, kx=0):
        pairs = [
            (i * bas + j, (i ^ kz) * bas + (j ^ kx)) for i in range(aux) for j in range(bas)
        ]
        return lax.ppermute(value, ("aux", "bas"), pairs)

    def across(value):
        return lax.ppermute(value, "occ", [(0, 1), (1, 0)])

    def after(value, *earlier):
        return lax.optimization_barrier((value, *earlier))[0]

    integrals = pltpu.with_memory_space_constraint(integrals, pltpu.HBM)
    other = swap(coefficients, kx=1)
    moved = relayout(integrals, first)
    where = jnp.concatenate([jnp.stack([a * bas + b, b]), screening[0, 0]]).astype(jnp.int32)
    rows = metric.shape[0] // 4
    held = lax.dynamic_slice_in_dim(metric, (b * 2 + o) * rows, rows, axis=0)
    held = [held, swap(held, kz=2)]
    *early, table = first_products(
        chips, where, after(coefficients, *held), other, moved, first
    )
    held = jnp.concatenate(held, axis=0)
    sent = []

    def send(value, kz, kx):
        if len(sent) >= WINDOW:
            value = after(value, sent[-WINDOW])
        sent.append(swap(value, kz, kx))
        return sent[-1]

    got = {(k, -1): send(early[k], k // bas, k % bas) for k in OPEN}
    got[0, -1] = early[0]
    spans = [(k, lo, hi) for lo, hi in groups for k in outer]
    spans += [(k, 0, share) for k in (0, *inner)]
    late = rest_products(chips, tuple(spans), integrals, table, first, got[RESTDEP, -1])
    made = dict(zip(spans, late))
    got[0, 0] = made[0, 0, share]
    for k, g in ORDER:
        if g < 0:
            value = after(early[k], late[0])
        else:
            value = made[(k, *groups[g])] if k in outer else made[k, 0, share]
        got[k, g] = send(value, k // bas, k % bas)
    held = jnp.concatenate([held, swap(held, kz=1)], axis=0)
    held = jnp.concatenate([held, swap(held, kx=1)], axis=0)
    ordered = ordered_metric(
        jnp.concatenate([aux_owner, a[None]]).astype(jnp.int32), [held, across(held)]
    )
    early = [got[k, -1] for k in range(chips)]
    total = None
    for g, (lo, hi) in enumerate(groups):
        part = [
            (got[k, g], 0) if k in outer else (got[k, 0], lo) for k in range(chips)
        ]
        place = jnp.stack([a, b, o]).astype(jnp.int32) if g == len(groups) - 1 else None
        total = group(aux, bas, lo, hi, ordered, early, part, total, place)
    kept, near, kept_away, near_away = total
    near = near + across(near_away)
    near = swap(near, kx=1)
    kept = kept + across(kept_away)
    kept = kept + near
    value = kept[0]
    for kz in LAST:
        value = value + swap(kept[kz], kz=kz)
    return value.T


def plain_device(integrals, screening, coefficients, metric, aux_owner):
    block_size = integrals.shape[-1]
    aux_count = lax.axis_size("aux")
    bas_count = lax.axis_size("bas")
    occ_count = lax.axis_size("occ")
    gathered = lax.all_gather(coefficients, "bas", axis=0, tiled=True)
    orbitals = gathered.shape[1]
    by_block = gathered.reshape(gathered.shape[0] // block_size, block_size, orbitals)
    picked = jnp.take(by_block, screening[0, 0], axis=0)
    stacked = integrals[0, 0].reshape(integrals.shape[2], block_size, block_size * block_size)
    contracted = lax.dot_general(
        picked, stacked, (((0, 1), (0, 1)), ((), ())), preferred_element_type=jnp.float32
    )
    transformed = contracted.astype(jnp.bfloat16)
    share = orbitals // (aux_count * bas_count)
    moved = lax.all_to_all(
        transformed.reshape(orbitals, 1, block_size, block_size),
        ("aux", "bas"),
        split_axis=0,
        concat_axis=1,
        tiled=True,
    )
    moved = moved.reshape(share, aux_count, bas_count, block_size, block_size)
    aux_table = (aux_owner[:, None] == jnp.arange(aux_count, dtype=jnp.int32)[None, :]).astype(
        jnp.bfloat16
    )
    piece = lax.all_gather(metric, "aux", axis=0, tiled=True)
    columns = piece.reshape(piece.shape[0], aux_count, block_size)
    ordered = jnp.einsum(
        "rgp,ag->rap", columns, aux_table, preferred_element_type=jnp.float32
    ).astype(jnp.bfloat16)
    fitted = jnp.einsum(
        "rap,iabpm->irbm", ordered, moved, preferred_element_type=jnp.float32
    ).astype(jnp.bfloat16)
    partial_value = jnp.einsum(
        "iqbm,iqcn->bmcn", fitted, fitted, preferred_element_type=jnp.float32
    )
    column_share = bas_count * block_size // (aux_count * occ_count)
    arranged = partial_value.reshape(bas_count, block_size, aux_count, occ_count, column_share)
    arranged = arranged.transpose(2, 0, 3, 1, 4).reshape(-1, column_share)
    return lax.psum_scatter(arranged, ("aux", "bas", "occ"), scatter_dimension=0, tiled=True)


def solution(mesh):
    in_specs = (
        P(("parts", "aux"), "bas", None, None, None, None),
        P(("parts", "aux"), "bas", None),
        P(("parts", "bas"), "occ"),
        P(("parts", "aux"), None),
        P("parts"),
    )
    out_specs = P(("parts", "bas"), ("aux", "occ"))
    small = mesh.shape["aux"] == 4 and mesh.shape["bas"] == 2 and mesh.shape["occ"] == 2
    return jax.shard_map(
        per_device if small else plain_device,
        mesh=mesh,
        in_specs=in_specs,
        out_specs=out_specs,
        check_vma=False,
    )
```
